128 devices in a mesh: row: 8 (over y_hi, z), col: 16 (over x, y_lo, core).
Axes of the slice: x: 4, y: 4 (y_hi: 2, y_lo: 2; y = y_hi * 2 + y_lo), z: 4, core: 2. Of those that a mesh axis runs over, the one named last changes fastest.
Arguments:
- ancestor_inv: float32 [12288, 12288], P('row', 'col'), as said below
- lower_panel: float32 [12288, 4096], P(None, 'col'), may hold values from -1.5 to 1.5
- diag_block_inv: float32 [32, 128, 128], P('col', 'row'), as said below
- pattern: int32 [96, 32], replicated, may hold values 0 or 1
Outputs:
- off_inv: float32 [4096, 12288], P('col', 'row')
- diag_inv: float32 [32, 128, 128], P('col', 'row')
The draws below stay inside these ranges and needn't reach their ends.
Inputs may be any that keep to these rules, and one draw needn't show every extreme that they name: ancestor_inv is symmetric. Each supernode's block of diag_block_inv is symmetric.
All inputs are finite; a program needn't handle non-finite values.
Results may differ from the reference program's by a relative error of at most 0.00007.
Values sent between devices are 32-bit elements; how exact they have to be, the bound alone decides.
A program may use at most 256 MiB of HBM per device.

```python
import math
import jax
import jax.numpy as jnp
from jax import lax

SUPER = 128
ORDER = 12288
NODES = 32
NBLOCKS = 96


def draw_ancestor_inv(key, part):
    key = jax.random.fold_in(key, 11)
    base = jax.random.normal(key, (ORDER, ORDER), jnp.float32)
    return (base + jnp.transpose(base)) * (0.70710678 / math.sqrt(ORDER))


def draw_diag_block_inv(key, part):
    key = jax.random.fold_in(key, 23)
    base = jax.random.normal(key, (NODES, SUPER, SUPER), jnp.float32)
    return (base + jnp.swapaxes(base, 1, 2)) * 0.70710678


def place_ends(array, key, smallest, top_value):
    index_at = [jax.random.randint(jax.random.fold_in(key, axis), (), 0, length) for axis, length in enumerate(array.shape)]
    widest = array.shape.index(max(array.shape))
    next_to = index_at[:widest] + [(index_at[widest] + 1) % array.shape[widest]] + index_at[widest + 1:]
    return array.at[tuple(index_at)].set(smallest).at[tuple(next_to)].set(top_value)


def level_of(key, dims, pieces, smallest, largest):
    loudness = 1.0
    for axis_at, blocks in pieces:
        steps = jax.random.uniform(jax.random.fold_in(jax.random.fold_in(key, 6), axis_at), (blocks,), jnp.float32, smallest / len(pieces), largest / len(pieces))
        loudness = loudness * jnp.repeat(jnp.exp(steps), dims[axis_at] // blocks).reshape((-1,) + (1,) * (len(dims) - 1 - axis_at))
    return loudness


def scatter_about(stream_key, shape, spread, reach, pieces=(), held_as=jnp.bfloat16):
    array = spread * jax.random.normal(stream_key, shape, jnp.float32)
    if pieces:
        array = array * level_of(stream_key, shape, pieces, -0.22, 0.18)
    return jnp.clip(array, -reach, reach).astype(held_as)


def setup_inputs(seed: int = 0) -> dict:
    streams_of = jax.random.split(jax.random.key(seed), 5)
    ancestor_inv = draw_ancestor_inv(jax.random.fold_in(streams_of[4], 71), 0)
    lower_panel = scatter_about(streams_of[1], (ORDER, NODES * SUPER), 0.25, 1.5, ((1, 16),), jnp.float32)
    diag_block_inv = draw_diag_block_inv(jax.random.fold_in(streams_of[4], 71), 0)
    pattern = place_ends((jax.random.randint(streams_of[3], (NBLOCKS, NODES), 0, 2) < 1).astype(jnp.int32), jax.random.fold_in(streams_of[3], 1), 0, 1)
    return {"ancestor_inv": ancestor_inv, "lower_panel": lower_panel, "diag_block_inv": diag_block_inv, "pattern": pattern}


def apply_pattern(panel, pattern):
    full_rows, width_all = panel.shape
    block_count = full_rows // SUPER
    node_count = width_all // SUPER
    kept_mask = pattern.astype(jnp.float32)[:, None, :, None]
    return (panel.reshape(block_count, SUPER, node_count, SUPER) * kept_mask).reshape(full_rows, width_all)


def reference(ancestor_inv, lower_panel, diag_block_inv, pattern):
    full_rows, width_all = lower_panel.shape
    block_count = full_rows // SUPER
    node_count = width_all // SUPER
    masked = apply_pattern(lower_panel, pattern)
    product = lax.dot_general(masked, ancestor_inv, (((0,), (1,)), ((), ())), precision=lax.Precision.HIGHEST, preferred_element_type=jnp.float32)
    kept_mask = jnp.transpose(pattern).astype(jnp.float32)[:, None, :, None]
    off_inv = -(product.reshape(node_count, SUPER, block_count, SUPER) * kept_mask).reshape(width_all, full_rows)
    blocks = product.reshape(node_count, SUPER, full_rows)
    panels = masked.reshape(full_rows, node_count, SUPER)
    diag_inv = diag_block_inv + jnp.einsum("kbg,gkm->kbm", blocks, panels, precision=lax.Precision.HIGHEST, preferred_element_type=jnp.float32)
    return (off_inv, diag_inv)
```

```python
import jax
import jax.numpy as jnp
from jax import lax
from jax.sharding import PartitionSpec as P

SUPER = 128


def body(rows, cols, ancestor_inv, lower_panel, diag_block_inv, pattern):
    rows_here, cols_here = ancestor_inv.shape
    full_rows, width_here = lower_panel.shape
    node_count = width_here // SUPER
    row_blocks = rows_here // SUPER
    col_index = lax.axis_index("col")
    row_index = lax.axis_index("row")
    kept = lax.dynamic_slice(
        pattern, (row_index * row_blocks, col_index * node_count), (row_blocks, node_count)
    ).astype(jnp.float32)
    panel_rows = lax.dynamic_slice_in_dim(lower_panel, row_index * rows_here, rows_here, 0)
    masked = (
        panel_rows.reshape(row_blocks, SUPER, node_count, SUPER) * kept[:, None, :, None]
    ).reshape(rows_here, width_here)
    gathered = lax.all_gather(masked, "col", axis=1, tiled=True)
    partial = lax.dot_general(
        gathered,
        ancestor_inv,
        (((0,), (0,)), ((), ())),
        precision=lax.Precision.HIGH,
        preferred_element_type=jnp.float32,
    )
    summed = lax.psum_scatter(partial, "row", scatter_dimension=0, tiled=True)
    odd = col_index % 2
    same, other = [], []
    for r in range(rows):
        for c in range(cols):
            same.append((r * cols + c, (c // 2) * cols + 2 * r + c % 2))
            other.append((r * cols + c, (c // 2) * cols + 2 * r + 1 - c % 2))
    keep_part = lax.dynamic_slice_in_dim(summed, odd * width_here, width_here, 0)
    swap_part = lax.dynamic_slice_in_dim(summed, (1 - odd) * width_here, width_here, 0)
    keep_part = lax.ppermute(keep_part, ("row", "col"), same)
    swap_part = lax.ppermute(swap_part, ("row", "col"), other)
    product = jnp.where(
        odd == 0,
        jnp.concatenate([keep_part, swap_part], 1),
        jnp.concatenate([swap_part, keep_part], 1),
    )
    off_inv = -(
        product.reshape(node_count, SUPER, row_blocks, SUPER) * jnp.transpose(kept)[:, None, :, None]
    ).reshape(width_here, rows_here)
    partial_diag = jnp.einsum(
        "kbg,gkm->kbm",
        product.reshape(node_count, SUPER, rows_here),
        masked.reshape(rows_here, node_count, SUPER),
        precision=lax.Precision.HIGHEST,
        preferred_element_type=jnp.float32,
    )
    diag_inv = diag_block_inv + lax.psum_scatter(partial_diag, "row", scatter_dimension=1, tiled=True)
    return (off_inv, diag_inv)


def solution(mesh):
    rows, cols = mesh.shape["row"], mesh.shape["col"]
    in_specs = (P("row", "col"), P(None, "col"), P("col", "row", None), P())
    out_specs = (P("col", "row"), P("col", "row", None))

    def local(*args):
        return body(rows, cols, *args)

    return jax.shard_map(local, mesh=mesh, in_specs=in_specs, out_specs=out_specs, check_vma=False)
```

```python
import functools

import jax
import jax.numpy as jnp
from jax import lax
from jax.experimental import pallas as pl
from jax.experimental.pallas import tpu as pltpu
from jax.sharding import PartitionSpec as P

SUPER = 128
MESH = pl.DeviceIdType.MESH
RING = 4
EVENTS = 16


def arrivals():
    table = [[(0, 0, 0, 0), (0, 0, 0, 1)], [(0, 0, 1, 0), (0, 0, 1, 1)]]
    for half in range(2):
        table.append([(0, 1, 0, half), (0, 1, 1, half)])
        for core in range(2):
            table.append([(-1, 0, core, half), (1, 0, core, half)])
    for half in range(2):
        for core in range(2):
            table.append([(-1, 1, core, half), (1, 1, core, half)])
    for dy in range(2):
        for core in range(2):
            table.append([(2, dy, core, 0), (2, dy, core, 1)])
    return table


TABLE = arrivals()
PLACE = {unit: (event, slot) for event, pair in enumerate(TABLE) for slot, unit in enumerate(pair)}


def forwards(unit):
    dx, dy, core, half = unit
    if core:
        return []
    out = []
    if dx == 0:
        if dy == 0:
            out.append(("y", (0, 1, 0, half)))
        out.append(("x+", (-1, dy, 0, half)))
        out.append(("x-", (1, dy, 0, half)))
    if dx == -1 and half == 0:
        out.append(("x+", (2, dy, 0, half)))
    if dx == 1 and half == 1:
        out.append(("x-", (2, dy, 0, half)))
    out.append(("core", (dx, dy, 1, half)))
    return out


SENDS = {}
for _pair in TABLE:
    for _unit in _pair:
        for _way, _name in forwards(_unit):
            SENDS[(_unit, _way)] = len(SENDS)


def split(value):
    high = value.astype(jnp.bfloat16)
    low = (value - high.astype(jnp.float32)).astype(jnp.bfloat16)
    return high, low


def kernel(
    kept, panel, ancestor, diag, off, diag_out,
    gathered, a_high, a_low, m_high, m_low, product, first, second, third, full, home, a_chunk, mine, theirs,
    load_sem, a_sem, gather_send, gather_recv, part_send, part_recv, home_send, home_recv, diag_send, diag_recv,
):
    row, col = lax.axis_index("row"), lax.axis_index("col")
    y_hi, z = row // RING, lax.rem(row, RING)
    x, y_lo, core = col // 4, lax.rem(col // 2, 2), lax.rem(col, 2)
    depth = panel.shape[1]
    width = ancestor.shape[1]
    piece = width // 8
    chip = col // 2

    def col_at(dx, dy, dcore):
        nx = lax.rem(x + (dx + RING), RING)
        ny = 1 - y_lo if dy else y_lo
        nc = 1 - core if dcore else core
        return nx * 4 + ny * 2 + nc

    def row_at(dyh, dz):
        nz = lax.rem(z + (dz + RING), RING)
        return (1 - y_hi if dyh else y_hi) * RING + nz

    ways = {
        "x+": (row, col_at(1, 0, 0)),
        "x-": (row, col_at(-1, 0, 0)),
        "y": (row, col_at(0, 1, 0)),
        "core": (row, col_at(0, 0, 1)),
        "z+": (row_at(0, 1), col),
        "z-": (row_at(0, -1), col),
        "yh": (row_at(1, 0), col),
    }

    def loads():
        return [
            pltpu.make_async_copy(panel.at[half], gathered.at[0, half], load_sem.at[half]) for half in range(2)
        ]

    def a_load(step, slot):
        rows = pl.ds(pl.multiple_of(step * SUPER, SUPER), SUPER)
        return pltpu.make_async_copy(ancestor.at[rows], a_chunk.at[slot], a_sem.at[slot])

    for copy in loads():
        copy.start()
    a_load(0, 0).start()

    barrier = pltpu.get_barrier_semaphore()

    def greet(device):
        pl.semaphore_signal(barrier, inc=1, device_id=device, device_id_type=MESH)

    for device in ways.values():
        greet(device)
    for step in range(1, 8):
        greet((lax.rem(row + step, 8), col))
    home_row = chip

    def greet_sources(step, carry):
        source_row, source_col = step // 2, 2 * row + lax.rem(step, 2)

        @pl.when(jnp.logical_or(source_row != row, source_col != col))
        def _():
            greet((source_row, source_col))

        return carry

    lax.fori_loop(0, 16, greet_sources, 0)
    pl.semaphore_wait(barrier, len(ways) + 7 + 16 - (home_row == row).astype(jnp.int32))

    def gather_copy(unit, way):
        name = dict(forwards(unit))[way]
        event, slot = PLACE[unit]
        to_event, to_slot = PLACE[name]
        return pltpu.make_async_remote_copy(
            src_ref=gathered.at[event, slot],
            dst_ref=gathered.at[to_event, to_slot],
            send_sem=gather_send.at[SENDS[(unit, way)]],
            recv_sem=gather_recv.at[to_event, to_slot],
            device_id=ways[way],
            device_id_type=MESH,
        )

    def arrived(event, slot):
        return pltpu.make_async_remote_copy(
            src_ref=gathered.at[event, slot],
            dst_ref=gathered.at[event, slot],
            send_sem=gather_send.at[0],
            recv_sem=gather_recv.at[event, slot],
            device_id=ways["core"],
            device_id_type=MESH,
        )

    for copy in loads():
        copy.wait()
    for unit in TABLE[0]:
        for way, _ in forwards(unit):
            gather_copy(unit, way).start()

    def convert(step, carry):
        slot = lax.rem(step, 2)

        @pl.when(step + 1 < depth // SUPER)
        def _():
            a_load(step + 1, 1 - slot).start()

        a_load(step, slot).wait()
        high, low = split(a_chunk[slot].T)
        lanes = pl.ds(pl.multiple_of(step * SUPER, SUPER), SUPER)
        a_high[:, lanes] = high
        a_low[:, lanes] = low
        return carry

    lax.fori_loop(0, depth // SUPER, convert, 0)

    def compute(event):
        def prepare(step, carry):
            rows = pl.ds(pl.multiple_of(step * 256, 256), 256)
            for slot in range(2):
                high, low = split(gathered[event, slot, rows, :])
                m_high[rows, slot * SUPER:(slot + 1) * SUPER] = high
                m_low[rows, slot * SUPER:(slot + 1) * SUPER] = low
            return carry

        lax.fori_loop(0, depth // 256, prepare, 0)

        def multiply(step, carry):
            rows = pl.ds(pl.multiple_of(step * (width // 2), width // 2), width // 2)
            high = a_high[rows, :]
            total = jnp.dot(high, m_low[...], preferred_element_type=jnp.float32)
            total += jnp.dot(a_low[rows, :], m_high[...], preferred_element_type=jnp.float32)
            total += jnp.dot(high, m_high[...], preferred_element_type=jnp.float32)
            product[event, rows, :] = total
            return carry

        lax.fori_loop(0, 2, multiply, 0)

    def rows_of(part, dz):
        target = lax.rem(z + (dz + RING), RING) + part * RING
        return pl.ds(pl.multiple_of(target * piece, 8), piece)

    def part_copy(event, index, source, target, recv, way):
        return pltpu.make_async_remote_copy(
            src_ref=source,
            dst_ref=target,
            send_sem=part_send.at[event, index],
            recv_sem=part_recv.at[event, recv],
            device_id=ways[way],
            device_id_type=MESH,
        )

    def copies(event):
        block = product.at[event]
        make = {
            "far_a": lambda: part_copy(event, 0, block.at[rows_of(0, 2)], first.at[event, 0], 0, "z-"),
            "far_b": lambda: part_copy(event, 1, block.at[rows_of(1, 2)], first.at[event, 1], 1, "z+"),
            "near_a": lambda: part_copy(event, 2, block.at[rows_of(0, 1)], second.at[event, 0], 2, "z+"),
            "near_b": lambda: part_copy(event, 3, block.at[rows_of(1, -1)], second.at[event, 1], 3, "z-"),
            "sum_a": lambda: part_copy(event, 4, first.at[event, 0], second.at[event, 2], 4, "z-"),
            "sum_b": lambda: part_copy(event, 5, first.at[event, 1], second.at[event, 3], 5, "z+"),
            "yh": lambda: part_copy(
                event, 6,
                block.at[pl.ds(pl.multiple_of(((1 - y_hi) * RING + z) * piece, 8), piece)],
                third.at[event], 6, "yh",
            ),
        }
        return make

    def stage_send(event):
        table = copies(event)
        for name in ("far_a", "far_b", "near_a", "near_b"):
            table[name]().start()

    def stage_pass(event):
        table = copies(event)
        table["far_a"]().wait_recv()
        first[event, 0] = first[event, 0] + product[event, rows_of(0, -1), :]
        table["sum_a"]().start()
        table["far_b"]().wait_recv()
        first[event, 1] = first[event, 1] + product[event, rows_of(1, 1), :]
        table["sum_b"]().start()

    def stage_cross(event):
        table = copies(event)
        for name in ("near_a", "near_b", "sum_a", "sum_b"):
            table[name]().wait_recv()
        for part in range(2):
            rows = rows_of(part, 0)
            product[event, rows, :] = product[event, rows, :] + second[event, part] + second[event, part + 2]
        table["yh"]().start()

    home_rows = pl.ds(pl.multiple_of(lax.rem(col, 2) * width + row * piece, 8), piece)

    def home_copy(event, slot):
        dx, dy, dcore, half = TABLE[event][slot]
        target = col_at(dx, dy, dcore)
        recv = home_recv.at[lax.rem(col, 2) * 16 + row * 2 + half]
        return pltpu.make_async_remote_copy(
            src_ref=full.at[event, slot],
            dst_ref=home.at[half, home_rows],
            send_sem=home_send.at[event, slot],
            recv_sem=recv,
            device_id=(home_row, target),
            device_id_type=MESH,
        )

    def stays(event, slot):
        half = TABLE[event][slot][3]
        return pltpu.make_async_copy(
            full.at[event, slot],
            home.at[half, home_rows],
            home_recv.at[lax.rem(col, 2) * 16 + row * 2 + half],
        )

    def stage_home(event):
        copies(event)["yh"]().wait_recv()
        total = product[event, pl.ds(pl.multiple_of(row * piece, 8), piece), :] + third[event]
        for slot in range(2):
            full[event, slot] = total[:, slot * SUPER:(slot + 1) * SUPER]
            if TABLE[event][slot][:3] == (0, 0, 0):

                @pl.when(home_row != row)
                def _():
                    home_copy(event, slot).start()

                @pl.when(home_row == row)
                def _():
                    stays(event, slot).start()
            else:
                home_copy(event, slot).start()

    for event in range(EVENTS + 3):
        if event < EVENTS:
            for slot, unit in enumerate(TABLE[event]):
                if event > 0:
                    arrived(event, slot).wait_recv()
                    for way, _ in forwards(unit):
                        gather_copy(unit, way).start()
            compute(event)
            stage_send(event)
        if 0 <= event - 1 < EVENTS:
            stage_pass(event - 1)
        if 0 <= event - 2 < EVENTS:
            stage_cross(event - 2)
        if 0 <= event - 3 < EVENTS:
            stage_home(event - 3)

    def home_wait(step, carry):
        side, source, half = step // 16, lax.rem(step // 2, 8), lax.rem(step, 2)
        rows = pl.ds(pl.multiple_of(side * width + source * piece, 8), piece)
        pltpu.make_async_copy(home.at[half, rows], home.at[half, rows], home_recv.at[step]).wait()
        return carry

    lax.fori_loop(0, 32, home_wait, 0)

    blocks = depth // SUPER
    for half in range(2):
        total = jnp.zeros((SUPER, SUPER), jnp.float32)
        for block in range(blocks):
            rows = slice(block * SUPER, (block + 1) * SUPER)
            tile = home[half, rows, :].T
            off[half * SUPER:(half + 1) * SUPER, rows] = tile * (-kept[block, half])
            t_high, t_low = split(tile)
            p_high, p_low = split(gathered[0, half, rows, :])
            total += jnp.dot(t_high, p_low, preferred_element_type=jnp.float32)
            total += jnp.dot(t_low, p_high, preferred_element_type=jnp.float32)
            total += jnp.dot(t_high, p_high, preferred_element_type=jnp.float32)
        share = SUPER // 8
        for target in range(8):
            mine[target, half] = total[target * share:(target + 1) * share]

    def diag_copy(step):
        target = lax.rem(row + step, 8)
        return pltpu.make_async_remote_copy(
            src_ref=mine.at[target],
            dst_ref=theirs.at[step],
            send_sem=diag_send.at[step],
            recv_sem=diag_recv.at[step],
            device_id=(target, col),
            device_id_type=MESH,
        )

    for step in range(1, 8):
        diag_copy(step).start()
    total = diag[...] + mine[row]
    for step in range(1, 8):
        diag_copy(step).wait_recv()
        total += theirs[step]
    diag_out[...] = total

    for step in range(1, 8):
        diag_copy(step).wait_send()
    for (unit, way) in SENDS:
        gather_copy(unit, way).wait_send()
    for event in range(EVENTS):
        for make in copies(event).values():
            make().wait_send()
        for slot in range(2):
            if TABLE[event][slot][:3] == (0, 0, 0):

                @pl.when(home_row != row)
                def _():
                    home_copy(event, slot).wait_send()
            else:
                home_copy(event, slot).wait_send()


def body(ancestor_inv, lower_panel, diag_block_inv, pattern):
    depth, width = ancestor_inv.shape
    width_here = lower_panel.shape[1]
    node_count = width_here // SUPER
    row_blocks = depth // SUPER
    col_index = lax.axis_index("col")
    row_index = lax.axis_index("row")
    kept = lax.dynamic_slice(
        pattern, (row_index * row_blocks, col_index * node_count), (row_blocks, node_count)
    ).astype(jnp.float32)
    panel_rows = lax.dynamic_slice_in_dim(lower_panel, row_index * depth, depth, 0)
    masked = panel_rows.reshape(row_blocks, SUPER, node_count, SUPER) * kept[:, None, :, None]
    units = jnp.transpose(masked.reshape(depth, node_count, SUPER), (1, 0, 2))
    piece = width // 8
    share = SUPER // 8
    f32, bf16 = jnp.float32, jnp.bfloat16
    off, diag = pl.pallas_call(
        kernel,
        out_shape=(
            jax.ShapeDtypeStruct((width_here, depth), f32),
            jax.ShapeDtypeStruct(diag_block_inv.shape, f32),
        ),
        in_specs=[
            pl.BlockSpec(memory_space=pltpu.SMEM),
            pl.BlockSpec(memory_space=pl.ANY),
            pl.BlockSpec(memory_space=pl.ANY),
            pl.BlockSpec(memory_space=pltpu.VMEM),
        ],
        out_specs=(pl.BlockSpec(memory_space=pltpu.VMEM), pl.BlockSpec(memory_space=pltpu.VMEM)),
        scratch_shapes=[
            pltpu.VMEM((EVENTS, 2, depth, SUPER), f32),
            pltpu.VMEM((width, depth), bf16),
            pltpu.VMEM((width, depth), bf16),
            pltpu.VMEM((depth, 2 * SUPER), bf16),
            pltpu.VMEM((depth, 2 * SUPER), bf16),
            pltpu.VMEM((EVENTS, width, 2 * SUPER), f32),
            pltpu.VMEM((EVENTS, 2, piece, 2 * SUPER), f32),
            pltpu.VMEM((EVENTS, 4, piece, 2 * SUPER), f32),
            pltpu.VMEM((EVENTS, piece, 2 * SUPER), f32),
            pltpu.VMEM((EVENTS, 2, piece, SUPER), f32),
            pltpu.VMEM((2, depth, SUPER), f32),
            pltpu.VMEM((2, SUPER, width), f32),
            pltpu.VMEM((8, 2, share, SUPER), f32),
            pltpu.VMEM((8, 2, share, SUPER), f32),
            pltpu.SemaphoreType.DMA((2,)),
            pltpu.SemaphoreType.DMA((2,)),
            pltpu.SemaphoreType.DMA((len(SENDS),)),
            pltpu.SemaphoreType.DMA((EVENTS, 2)),
            pltpu.SemaphoreType.DMA((EVENTS, 7)),
            pltpu.SemaphoreType.DMA((EVENTS, 7)),
            pltpu.SemaphoreType.DMA((EVENTS, 2)),
            pltpu.SemaphoreType.DMA((32,)),
            pltpu.SemaphoreType.DMA((8,)),
            pltpu.SemaphoreType.DMA((8,)),
        ],
        compiler_params=pltpu.CompilerParams(
            collective_id=0, has_side_effects=True, vmem_limit_bytes=63 * 2**20
        ),
        cost_estimate=pl.CostEstimate(
            flops=6 * depth * width * 16 * 2 * SUPER, bytes_accessed=16 * 2**20, transcendentals=0
        ),
    )(kept, units, ancestor_inv, diag_block_inv)
    return (off, diag)


def solution(mesh):
    in_specs = (P("row", "col"), P(None, "col"), P("col", "row", None), P())
    out_specs = (P("col", "row"), P("col", "row", None))
    return jax.shard_map(body, mesh=mesh, in_specs=in_specs, out_specs=out_specs, check_vma=False)
```

```python
import functools

import jax
import jax.numpy as jnp
from jax import lax
from jax.experimental import pallas as pl
from jax.experimental.pallas import tpu as pltpu
from jax.sharding import PartitionSpec as P

SUPER = 128
MESH = pl.DeviceIdType.MESH
RING = 4
EVENTS = 16


def arrivals():
    table = [[(0, 0, 0, 0), (0, 0, 0, 1)], [(0, 0, 1, 0), (0, 0, 1, 1)]]
    for half in range(2):
        table.append([(0, 1, 0, half), (0, 1, 1, half)])
        for core in range(2):
            table.append([(-1, 0, core, half), (1, 0, core, half)])
    for half in range(2):
        for core in range(2):
            table.append([(-1, 1, core, half), (1, 1, core, half)])
    for dy in range(2):
        for core in range(2):
            table.append([(2, dy, core, 0), (2, dy, core, 1)])
    return table


TABLE = arrivals()
PLACE = {unit: (event, slot) for event, pair in enumerate(TABLE) for slot, unit in enumerate(pair)}


def forwards(unit):
    dx, dy, core, half = unit
    if core:
        return []
    out = []
    if dx == 0:
        if dy == 0:
            out.append(("y", (0, 1, 0, half)))
        out.append(("x+", (-1, dy, 0, half)))
        out.append(("x-", (1, dy, 0, half)))
    if dx == -1 and half == 0:
        out.append(("x+", (2, dy, 0, half)))
    if dx == 1 and half == 1:
        out.append(("x-", (2, dy, 0, half)))
    out.append(("core", (dx, dy, 1, half)))
    return out


SENDS = {}
for _pair in TABLE:
    for _unit in _pair:
        for _way, _name in forwards(_unit):
            SENDS[(_unit, _way)] = len(SENDS)


def split(value):
    high = value.astype(jnp.bfloat16)
    low = (value - high.astype(jnp.float32)).astype(jnp.bfloat16)
    return high, low


def kernel(
    pattern, panel, ancestor, diag, off, diag_out,
    gathered, a_high, a_low, m_high, m_low, product, first, second, third, full, relay, home, a_chunk, mine, theirs,
    load_sem, a_sem, gather_send, gather_recv, part_send, part_recv, relay_send, relay_recv, home_send, home_recv,
    diag_send, diag_recv,
):
    row, col = lax.axis_index("row"), lax.axis_index("col")
    y_hi, z = row // RING, lax.rem(row, RING)
    x, y_lo, core = col // 4, lax.rem(col // 2, 2), lax.rem(col, 2)
    depth, width = ancestor.shape
    blocks = depth // SUPER
    piece = width // 8

    def col_at(dx, dy, dcore):
        nx = lax.rem(x + (dx + RING), RING)
        ny = 1 - y_lo if dy else y_lo
        nc = 1 - core if dcore else core
        return nx * 4 + ny * 2 + nc

    def row_at(dyh, dz):
        nz = lax.rem(z + (dz + RING), RING)
        return (1 - y_hi if dyh else y_hi) * RING + nz

    ways = {
        "x+": (row, col_at(1, 0, 0)),
        "x-": (row, col_at(-1, 0, 0)),
        "y": (row, col_at(0, 1, 0)),
        "core": (row, col_at(0, 0, 1)),
        "z+": (row_at(0, 1), col),
        "z-": (row_at(0, -1), col),
        "yh": (row_at(1, 0), col),
    }

    def loads():
        rows = pl.ds(pl.multiple_of(row * depth, SUPER), depth)
        return [
            pltpu.make_async_copy(
                panel.at[rows, pl.ds(half * SUPER, SUPER)], gathered.at[0, half], load_sem.at[half]
            )
            for half in range(2)
        ]

    def kept(block, half):
        return pattern[row * blocks + block, col * 2 + half].astype(jnp.float32)

    def a_load(step, slot):
        rows = pl.ds(pl.multiple_of(step * SUPER, SUPER), SUPER)
        return pltpu.make_async_copy(ancestor.at[rows], a_chunk.at[slot], a_sem.at[slot])

    for copy in loads():
        copy.start()
    a_load(0, 0).start()

    barrier = pltpu.get_barrier_semaphore()

    def greet(device):
        pl.semaphore_signal(barrier, inc=1, device_id=device, device_id_type=MESH)

    for device in ways.values():
        greet(device)
    pl.semaphore_wait(barrier, len(ways))

    def gather_copy(unit, way):
        name = dict(forwards(unit))[way]
        event, slot = PLACE[unit]
        to_event, to_slot = PLACE[name]
        return pltpu.make_async_remote_copy(
            src_ref=gathered.at[event, slot],
            dst_ref=gathered.at[to_event, to_slot],
            send_sem=gather_send.at[SENDS[(unit, way)]],
            recv_sem=gather_recv.at[to_event, to_slot],
            device_id=ways[way],
            device_id_type=MESH,
        )

    def arrived(event, slot):
        return pltpu.make_async_remote_copy(
            src_ref=gathered.at[event, slot],
            dst_ref=gathered.at[event, slot],
            send_sem=gather_send.at[0],
            recv_sem=gather_recv.at[event, slot],
            device_id=ways["core"],
            device_id_type=MESH,
        )

    for half, unit in enumerate(TABLE[0]):
        loads()[half].wait()

        def mask(block, carry):
            rows = pl.ds(pl.multiple_of(block * SUPER, SUPER), SUPER)
            gathered[0, half, rows, :] = gathered[0, half, rows, :] * kept(block, half)
            return carry

        lax.fori_loop(0, blocks, mask, 0)
        for way, _ in forwards(unit):
            gather_copy(unit, way).start()

    def convert(step, carry):
        slot = lax.rem(step, 2)

        @pl.when(step + 1 < depth // SUPER)
        def _():
            a_load(step + 1, 1 - slot).start()

        a_load(step, slot).wait()
        high, low = split(a_chunk[slot].T)
        lanes = pl.ds(pl.multiple_of(step * SUPER, SUPER), SUPER)
        a_high[:, lanes] = high
        a_low[:, lanes] = low
        return carry

    lax.fori_loop(0, depth // SUPER, convert, 0)

    def compute(event):
        def prepare(step, carry):
            rows = pl.ds(pl.multiple_of(step * 256, 256), 256)
            for slot in range(2):
                high, low = split(gathered[event, slot, rows, :])
                m_high[rows, slot * SUPER:(slot + 1) * SUPER] = high
                m_low[rows, slot * SUPER:(slot + 1) * SUPER] = low
            return carry

        lax.fori_loop(0, depth // 256, prepare, 0)

        def multiply(step, carry):
            rows = pl.ds(pl.multiple_of(step * (width // 2), width // 2), width // 2)
            high = a_high[rows, :]
            total = jnp.dot(high, m_low[...], preferred_element_type=jnp.float32)
            total += jnp.dot(a_low[rows, :], m_high[...], preferred_element_type=jnp.float32)
            total += jnp.dot(high, m_high[...], preferred_element_type=jnp.float32)
            product[event, rows, :] = total
            return carry

        lax.fori_loop(0, 2, multiply, 0)

    def rows_of(part, dz):
        target = lax.rem(z + (dz + RING), RING) + part * RING
        return pl.ds(pl.multiple_of(target * piece, 8), piece)

    def part_copy(event, index, source, target, recv, way):
        return pltpu.make_async_remote_copy(
            src_ref=source,
            dst_ref=target,
            send_sem=part_send.at[event, index],
            recv_sem=part_recv.at[event, recv],
            device_id=ways[way],
            device_id_type=MESH,
        )

    def copies(event):
        block = product.at[event]
        make = {
            "far_a": lambda: part_copy(event, 0, block.at[rows_of(0, 2)], first.at[event, 0], 0, "z-"),
            "far_b": lambda: part_copy(event, 1, block.at[rows_of(1, 2)], first.at[event, 1], 1, "z+"),
            "near_a": lambda: part_copy(event, 2, block.at[rows_of(0, 1)], second.at[event, 0], 2, "z+"),
            "near_b": lambda: part_copy(event, 3, block.at[rows_of(1, -1)], second.at[event, 1], 3, "z-"),
            "sum_a": lambda: part_copy(event, 4, first.at[event, 0], second.at[event, 2], 4, "z-"),
            "sum_b": lambda: part_copy(event, 5, first.at[event, 1], second.at[event, 3], 5, "z+"),
            "yh": lambda: part_copy(
                event, 6,
                block.at[pl.ds(pl.multiple_of(((1 - y_hi) * RING + z) * piece, 8), piece)],
                third.at[event], 6, "yh",
            ),
        }
        return make

    def stage_send(event):
        table = copies(event)
        for name in ("far_a", "far_b", "near_a", "near_b"):
            table[name]().start()

    def stage_pass(event):
        table = copies(event)
        table["far_a"]().wait_recv()
        first[event, 0] = first[event, 0] + product[event, rows_of(0, -1), :]
        table["sum_a"]().start()
        table["far_b"]().wait_recv()
        first[event, 1] = first[event, 1] + product[event, rows_of(1, 1), :]
        table["sum_b"]().start()

    def stage_cross(event):
        table = copies(event)
        for name in ("near_a", "near_b", "sum_a", "sum_b"):
            table[name]().wait_recv()
        for part in range(2):
            rows = rows_of(part, 0)
            product[event, rows, :] = product[event, rows, :] + second[event, part] + second[event, part + 2]
        table["yh"]().start()

    def relay_copy(event, slot):
        dx, dy, dcore, _ = TABLE[event][slot]
        return pltpu.make_async_remote_copy(
            src_ref=full.at[event, slot],
            dst_ref=relay.at[event, slot],
            send_sem=relay_send.at[event, slot],
            recv_sem=relay_recv.at[event, slot],
            device_id=(row, col_at(dx, dy, dcore)),
            device_id_type=MESH,
        )

    def home_step(event, slot, wait_only=False):
        dx, dy, dcore, half = TABLE[event][slot]
        source_col = col_at(-dx, dy, dcore)
        target_row = source_col // 2
        rows = pl.ds(pl.multiple_of(lax.rem(source_col, 2) * width + row * piece, 8), piece)
        source = (full if (dx, dy, dcore) == (0, 0, 0) else relay).at[event, slot]
        recv = home_recv.at[lax.rem(source_col, 2) * 16 + row * 2 + half]
        remote = target_row != row

        @pl.when(remote)
        def _():
            copy = pltpu.make_async_remote_copy(
                src_ref=source,
                dst_ref=home.at[half, rows],
                send_sem=home_send.at[event, slot],
                recv_sem=recv,
                device_id=(target_row, col),
                device_id_type=MESH,
            )
            if wait_only:
                copy.wait_send()
            else:
                copy.start()

        if not wait_only:

            @pl.when(jnp.logical_not(remote))
            def _():
                pltpu.make_async_copy(source, home.at[half, rows], recv).start()

    def stage_relay(event):
        copies(event)["yh"]().wait_recv()
        total = product[event, pl.ds(pl.multiple_of(row * piece, 8), piece), :] + third[event]
        for slot in range(2):
            full[event, slot] = total[:, slot * SUPER:(slot + 1) * SUPER]
            if TABLE[event][slot][:3] != (0, 0, 0):
                relay_copy(event, slot).start()

    def stage_home(event):
        for slot in range(2):
            if TABLE[event][slot][:3] != (0, 0, 0):
                relay_copy(event, slot).wait_recv()
            home_step(event, slot)

    for event in range(EVENTS + 4):
        if event < EVENTS:
            for slot, unit in enumerate(TABLE[event]):
                if event > 0:
                    arrived(event, slot).wait_recv()
                    for way, _ in forwards(unit):
                        gather_copy(unit, way).start()
            compute(event)
            stage_send(event)
        if 0 <= event - 1 < EVENTS:
            stage_pass(event - 1)
        if 0 <= event - 2 < EVENTS:
            stage_cross(event - 2)
        if 0 <= event - 3 < EVENTS:
            stage_relay(event - 3)
        if 0 <= event - 4 < EVENTS:
            stage_home(event - 4)

    def home_wait(step, carry):
        side, source, half = step // 16, lax.rem(step // 2, 8), lax.rem(step, 2)
        rows = pl.ds(pl.multiple_of(side * width + source * piece, 8), piece)
        pltpu.make_async_copy(home.at[half, rows], home.at[half, rows], home_recv.at[step]).wait()
        return carry

    lax.fori_loop(0, 32, home_wait, 0)

    for half in range(2):
        total = jnp.zeros((SUPER, SUPER), jnp.float32)
        for block in range(blocks):
            rows = slice(block * SUPER, (block + 1) * SUPER)
            tile = home[half, rows, :].T
            off[half * SUPER:(half + 1) * SUPER, rows] = tile * (-kept(block, half))
            t_high, t_low = split(tile)
            p_high, p_low = split(gathered[0, half, rows, :])
            total += jnp.dot(t_high, p_low, preferred_element_type=jnp.float32)
            total += jnp.dot(t_low, p_high, preferred_element_type=jnp.float32)
            total += jnp.dot(t_high, p_high, preferred_element_type=jnp.float32)
        share = SUPER // 8
        for target in range(8):
            mine[target, half] = total[target * share:(target + 1) * share]

    def diag_copy(step):
        target = lax.rem(row + step, 8)
        return pltpu.make_async_remote_copy(
            src_ref=mine.at[target],
            dst_ref=theirs.at[step],
            send_sem=diag_send.at[step],
            recv_sem=diag_recv.at[step],
            device_id=(target, col),
            device_id_type=MESH,
        )

    for step in range(1, 8):
        diag_copy(step).start()
    total = diag[...] + mine[row]
    for step in range(1, 8):
        diag_copy(step).wait_recv()
        total += theirs[step]
    diag_out[...] = total

    for step in range(1, 8):
        diag_copy(step).wait_send()
    for (unit, way) in SENDS:
        gather_copy(unit, way).wait_send()
    for event in range(EVENTS):
        for make in copies(event).values():
            make().wait_send()
        for slot in range(2):
            if TABLE[event][slot][:3] != (0, 0, 0):
                relay_copy(event, slot).wait_send()
            home_step(event, slot, wait_only=True)


def body(ancestor_inv, lower_panel, diag_block_inv, pattern):
    depth, width = ancestor_inv.shape
    width_here = lower_panel.shape[1]
    piece = width // 8
    share = SUPER // 8
    f32, bf16 = jnp.float32, jnp.bfloat16
    off, diag = pl.pallas_call(
        kernel,
        out_shape=(
            jax.ShapeDtypeStruct((width_here, depth), f32),
            jax.ShapeDtypeStruct(diag_block_inv.shape, f32),
        ),
        in_specs=[
            pl.BlockSpec(memory_space=pltpu.SMEM),
            pl.BlockSpec(memory_space=pl.ANY),
            pl.BlockSpec(memory_space=pl.ANY),
            pl.BlockSpec(memory_space=pltpu.VMEM),
        ],
        out_specs=(pl.BlockSpec(memory_space=pltpu.VMEM), pl.BlockSpec(memory_space=pltpu.VMEM)),
        scratch_shapes=[
            pltpu.VMEM((EVENTS, 2, depth, SUPER), f32),
            pltpu.VMEM((width, depth), bf16),
            pltpu.VMEM((width, depth), bf16),
            pltpu.VMEM((depth, 2 * SUPER), bf16),
            pltpu.VMEM((depth, 2 * SUPER), bf16),
            pltpu.VMEM((EVENTS, width, 2 * SUPER), f32),
            pltpu.VMEM((EVENTS, 2, piece, 2 * SUPER), f32),
            pltpu.VMEM((EVENTS, 4, piece, 2 * SUPER), f32),
            pltpu.VMEM((EVENTS, piece, 2 * SUPER), f32),
            pltpu.VMEM((EVENTS, 2, piece, SUPER), f32),
            pltpu.VMEM((EVENTS, 2, piece, SUPER), f32),
            pltpu.VMEM((2, depth, SUPER), f32),
            pltpu.VMEM((2, SUPER, width), f32),
            pltpu.VMEM((8, 2, share, SUPER), f32),
            pltpu.VMEM((8, 2, share, SUPER), f32),
            pltpu.SemaphoreType.DMA((2,)),
            pltpu.SemaphoreType.DMA((2,)),
            pltpu.SemaphoreType.DMA((len(SENDS),)),
            pltpu.SemaphoreType.DMA((EVENTS, 2)),
            pltpu.SemaphoreType.DMA((EVENTS, 7)),
            pltpu.SemaphoreType.DMA((EVENTS, 7)),
            pltpu.SemaphoreType.DMA((EVENTS, 2)),
            pltpu.SemaphoreType.DMA((EVENTS, 2)),
            pltpu.SemaphoreType.DMA((EVENTS, 2)),
            pltpu.SemaphoreType.DMA((32,)),
            pltpu.SemaphoreType.DMA((8,)),
            pltpu.SemaphoreType.DMA((8,)),
        ],
        compiler_params=pltpu.CompilerParams(
            collective_id=0, has_side_effects=True, vmem_limit_bytes=63 * 2**20
        ),
        cost_estimate=pl.CostEstimate(
            flops=6 * depth * width * 16 * 2 * SUPER, bytes_accessed=16 * 2**20, transcendentals=0
        ),
    )(pattern, lower_panel, ancestor_inv, diag_block_inv)
    return (off, diag)


def solution(mesh):
    in_specs = (P("row", "col"), P(None, "col"), P("col", "row", None), P())
    out_specs = (P("col", "row"), P("col", "row", None))
    return jax.shard_map(body, mesh=mesh, in_specs=in_specs, out_specs=out_specs, check_vma=False)
```

```python
import jax
import jax.numpy as jnp
from jax import lax
from jax.experimental import pallas as pl
from jax.experimental.pallas import tpu as pltpu
from jax.sharding import PartitionSpec as P

SUPER = 128
MESH = pl.DeviceIdType.MESH
RING = 4
ROWS = 8
SHARE = 32

SOURCES = ((0, 0), (0, 1), (-1, 0), (1, 0), (-1, 1), (1, 1), (2, 0), (2, 1))
HEAD = tuple((dx, dy, place) for dx, place in ((2, (0, 0)), (1, (1, 0)), (-1, (0, 1)), (0, (1, 1))) for dy in range(2))


def forwards(source, half):
    dz, dy = SOURCES[source]
    out = []
    if dz == 0:
        if dy == 0:
            out.append(("yh", SOURCES.index((0, 1))))
        out.append(("z+", SOURCES.index((-1, dy))))
        out.append(("z-", SOURCES.index((1, dy))))
    if dz == -1 and half == 0:
        out.append(("z+", SOURCES.index((2, dy))))
    if dz == 1 and half == 1:
        out.append(("z-", SOURCES.index((2, dy))))
    out.append(("core", source))
    return out


SENDS = {}
for _source in range(ROWS):
    for _half in range(2):
        for _way, _ in forwards(_source, _half):
            SENDS[(_source, _half, _way)] = len(SENDS)

ORDER = (
    ("arrive", 0, 0),
    ("arrive", 0, 1),
    ("product", 0, 0),
    ("product", 0, 1),
    ("minus", 0),
    ("plus", 0),
    ("arrive", 2, 0),
    ("arrive", 3, 0),
    ("arrive", 1, 0),
    ("own", 0),
    ("product", 2, 0),
    ("product", 3, 0),
    ("product", 1, 0),
    ("minus", 2),
    ("pair", 0),
    ("arrive", 2, 1),
    ("arrive", 3, 1),
    ("arrive", 1, 1),
    ("product", 2, 1),
    ("minus", 3),
    ("plus", 2),
    ("product", 3, 1),
    ("plus", 3),
    ("product", 1, 1),
    ("minus", 1),
    ("plus", 1),
    ("arrive", 5, 0),
    ("arrive", 6, 0),
    ("product", 5, 0),
    ("product", 6, 0),
    ("own", 2),
    ("own", 3),
    ("arrive", 4, 0),
    ("arrive", 6, 1),
    ("pair", 2),
    ("minus", 5),
    ("own", 1),
    ("pair", 3),
    ("product", 4, 0),
    ("product", 6, 1),
    ("minus", 6),
    ("plus", 6),
    ("pair", 1),
    ("arrive", 4, 1),
    ("arrive", 5, 1),
    ("product", 4, 1),
    ("minus", 4),
    ("plus", 4),
    ("product", 5, 1),
    ("plus", 5),
    ("own", 6),
    ("arrive", 7, 0),
    ("own", 4),
    ("arrive", 7, 1),
    ("pair", 6),
    ("product", 7, 0),
    ("product", 7, 1),
    ("own", 5),
    ("pair", 4),
    ("minus", 7),
    ("plus", 7),
    ("pair", 5),
    ("own", 7),
    ("pair", 7),
)


def split(value):
    high = value.astype(jnp.bfloat16)
    low = (value - high.astype(jnp.float32)).astype(jnp.bfloat16)
    return high, low


def kernel(
    pattern, panel, ancestor, diag, off, diag_out,
    gathered, a_high, a_low, m_high, m_low, product, far, near, crossed, result, chunk, turned, pieces, mine, theirs,
    chunk_sem, a_sem, a_send, a_recv, head_send, head_recv, gather_send, gather_recv, part_send, part_recv,
    core_send, core_recv, diag_send, diag_recv,
):
    row, col = lax.axis_index("row"), lax.axis_index("col")
    y_hi, z = row // RING, lax.rem(row, RING)
    x, y_lo, core = col // 4, lax.rem(col // 2, 2), lax.rem(col, 2)
    rows_here, cols_here = ancestor.shape
    depth = rows_here
    blocks = depth // SUPER
    half_rows = rows_here // 2

    def col_at(dx, dy, target_core):
        nx = lax.rem(x + (dx + RING), RING)
        ny = 1 - y_lo if dy else y_lo
        return nx * 4 + ny * 2 + target_core

    def row_at(dz, dy):
        nz = lax.rem(z + (dz + RING), RING)
        return (1 - y_hi if dy else y_hi) * RING + nz

    ways = {
        "x+": (row, col_at(1, 0, core)),
        "x-": (row, col_at(-1, 0, core)),
        "y": (row, col_at(0, 1, core)),
        "core": (row, col_at(0, 0, 1 - core)),
        "z+": (row_at(1, 0), col),
        "z-": (row_at(-1, 0), col),
        "yh": (row_at(0, 1), col),
    }

    def remote(source, target, send, recv, device):
        return pltpu.make_async_remote_copy(
            src_ref=source, dst_ref=target, send_sem=send, recv_sem=recv, device_id=device, device_id_type=MESH
        )

    barrier = pltpu.get_barrier_semaphore()

    def greet(device):
        pl.semaphore_signal(barrier, inc=1, device_id=device, device_id_type=MESH)

    def greet_row(step, carry):
        greet((row, lax.rem(col + step, 16)))
        return carry

    lax.fori_loop(1, 16, greet_row, 0)
    for way in ("z+", "z-", "yh"):
        greet(ways[way])

    def chunk_load(message):
        dx, dy, _ = HEAD[message]
        chip = col_at(dx, dy, 0) // 2
        rows = pl.ds(pl.multiple_of(chip * depth, SUPER), depth)
        lanes = pl.ds(pl.multiple_of((row // 4) * SUPER, SUPER), SUPER)
        return pltpu.make_async_copy(panel.at[rows, lanes], chunk.at[message % 2], chunk_sem.at[message % 2])

    def a_rows(which, part):
        return ancestor.at[pl.ds(pl.multiple_of(which * half_rows + part * 256, 256), 256)]

    own_place = ((2, 0), (2, 1), (3, 0))
    other_place = ((3, 1), (4, 0), (4, 1))

    def a_load(part):
        slot, half = own_place[part]
        return pltpu.make_async_copy(a_rows(core, part), product.at[slot, half], a_sem.at[part])

    def a_swap(part):
        slot, half = other_place[part]
        return remote(
            a_rows(1 - core, part), product.at[slot, half], a_send.at[part], a_recv.at[part], ways["core"]
        )

    chunk_load(0).start()
    chunk_load(1).start()
    for part in range(3):
        a_load(part).start()

    def kept(block_row, column):
        return pattern[block_row, column].astype(jnp.float32)

    def head_copy(message):
        dx, dy, (target_core, half) = HEAD[message]
        piece = y_lo * 2 + core
        return remote(
            pieces.at[message],
            gathered.at[0, target_core, half, pl.ds(pl.multiple_of(piece * SHARE, SHARE), SHARE)],
            head_send.at[message],
            head_recv.at[half, piece],
            (row, col_at(dx, dy, target_core)),
        )

    def head_stay(message):
        _, _, (target_core, half) = HEAD[message]
        piece = y_lo * 2 + core
        return pltpu.make_async_copy(
            pieces.at[message],
            gathered.at[0, target_core, half, pl.ds(pl.multiple_of(piece * SHARE, SHARE), SHARE)],
            head_recv.at[half, piece],
        )

    def stays(message):
        dx, dy, (target_core, _) = HEAD[message]
        return core == target_core if (dx, dy) == (0, 0) else None

    def turn(message):
        dx, dy, _ = HEAD[message]
        chip = col_at(dx, dy, 0) // 2
        chunk_load(message).wait()

        def block_turn(block, carry):
            rows = pl.ds(pl.multiple_of(block * SUPER, SUPER), SUPER)
            tile = chunk[message % 2, rows, :] * kept(chip * blocks + block, col * 2 + row // 4)
            turned[:, rows] = tile.T
            return carry

        lax.fori_loop(0, blocks, block_turn, 0, unroll=2)
        if message + 2 < len(HEAD):
            chunk_load(message + 2).start()
        pieces[message] = turned[pl.ds(pl.multiple_of(lax.rem(row, 4) * SHARE, SHARE), SHARE), :]

    turn(0)
    pl.semaphore_wait(barrier, 18)
    for part in range(3):
        a_swap(part).start()
    for message in range(len(HEAD)):
        if message > 0:
            turn(message)
        if stays(message) is None:
            head_copy(message).start()
        else:

            @pl.when(stays(message))
            def _():
                head_stay(message).start()

            @pl.when(jnp.logical_not(stays(message)))
            def _():
                head_copy(message).start()

    def convert(place, part, offset):
        slot, half = place[part]
        for step in range(2):
            for side in range(cols_here // 256):
                tile = product[slot, half, step * SUPER:(step + 1) * SUPER, side * 256:(side + 1) * 256].T
                high, low = split(tile)
                rows = pl.ds(pl.multiple_of(offset + side * 256, 256), 256)
                lanes = slice(part * 256 + step * SUPER, part * 256 + (step + 1) * SUPER)
                a_high[rows, lanes] = high
                a_low[rows, lanes] = low

    for part in range(3):
        a_load(part).wait()
        convert(own_place, part, core * cols_here)
    for part in range(3):
        a_swap(part).wait_recv()
        convert(other_place, part, (1 - core) * cols_here)

    def gather_copy(source, half, way):
        target = dict(forwards(source, half))[way]
        return remote(
            gathered.at[source, core, half],
            gathered.at[target, core, half],
            gather_send.at[SENDS[(source, half, way)]],
            gather_recv.at[target, core, half],
            ways[way],
        )

    def landed(source, which, half):
        place = gathered.at[source, which, half]
        pltpu.make_async_copy(place, place, gather_recv.at[source, which, half]).wait()

    def arrive(source, half):
        if source == 0:
            for piece in range(4):
                place = gathered.at[0, core, half, pl.ds(piece * SHARE, SHARE)]
                pltpu.make_async_copy(place, place, head_recv.at[half, piece]).wait()
        else:
            landed(source, core, half)
        for way, _ in forwards(source, half):
            gather_copy(source, half, way).start()

    def part_copy(source, index, block, target, way):
        return remote(block, target, part_send.at[source, index], part_recv.at[source, index], ways[way])

    def part(source, name):
        block = product.at[source]
        half = SUPER // 2
        if name == "far_a":
            return part_copy(source, 0, block.at[0, pl.ds(0, half)], far.at[source, 0], "x+")
        if name == "far_b":
            return part_copy(source, 1, block.at[0, pl.ds(half, half)], far.at[source, 1], "x-")
        if name == "minus_a":
            return part_copy(source, 2, block.at[0, pl.ds(2 * half, half)], near.at[source, 0], "x-")
        if name == "plus_b":
            return part_copy(source, 3, block.at[1, pl.ds(half, half)], near.at[source, 1], "x+")
        if name == "minus_b":
            return part_copy(source, 4, far.at[source, 1], near.at[source, 2], "x-")
        if name == "plus_a":
            return part_copy(source, 5, far.at[source, 0], near.at[source, 3], "x+")
        rows = pl.ds(pl.multiple_of(2 * half + (1 - y_lo) * half, half), half)
        return part_copy(source, 6, block.at[1, rows], crossed.at[source], "y")

    PARTS = ("far_a", "far_b", "minus_a", "plus_b", "minus_b", "plus_a", "cross")

    def multiply(source, half):
        landed(source, 1 - core, half)
        for which in range(2):
            def prepare(step, carry):
                rows = pl.ds(pl.multiple_of(step * 32, 32), 32)
                out = pl.ds(pl.multiple_of(which * SUPER + step * 32, 32), 32)
                high, low = split(gathered[source, which, half, rows, :])
                m_high[out, :] = high
                m_low[out, :] = low
                return carry

            lax.fori_loop(0, SUPER // 32, prepare, 0)

        def tile(step, carry):
            lanes = pl.ds(pl.multiple_of(step * 256, 256), 256)
            high = a_high[:, lanes]
            total = jnp.dot(m_low[...], high, preferred_element_type=jnp.float32)
            total += jnp.dot(m_high[...], a_low[:, lanes], preferred_element_type=jnp.float32)
            total += jnp.dot(m_high[...], high, preferred_element_type=jnp.float32)
            product[source, half, :, lanes] = total
            return carry

        lax.fori_loop(0, half_rows // 256, tile, 0)
        for name in ("far_a", "far_b", "minus_a") if half == 0 else ("plus_b",):
            part(source, name).start()

    def pass_on(source, which, half, first, arriving, leaving):
        part(source, arriving).wait_recv()
        count = SUPER // 2
        far[source, which] = far[source, which] + product[source, half, first:first + count, :]
        part(source, leaving).start()

    def own(source):
        count = SUPER // 2
        for name in ("minus_a", "plus_b", "minus_b", "plus_a"):
            part(source, name).wait_recv()
        product[source, 1, 2 * count:3 * count, :] = (
            product[source, 1, 2 * count:3 * count, :] + near[source, 0] + near[source, 3]
        )
        product[source, 1, 3 * count:, :] = product[source, 1, 3 * count:, :] + near[source, 1] + near[source, 2]
        part(source, "cross").start()

    def core_copy(source):
        where = row_at(*SOURCES[source])
        return remote(
            crossed.at[source, pl.ds(pl.multiple_of((1 - core) * SHARE, SHARE), SHARE)],
            result.at[core, pl.ds(pl.multiple_of(where * SHARE, SHARE), SHARE)],
            core_send.at[source],
            core_recv.at[where],
            ways["core"],
        )

    def pair(source):
        part(source, "cross").wait_recv()
        half = SUPER // 2
        rows = pl.ds(pl.multiple_of(2 * half + y_lo * half, half), half)
        crossed[source] = crossed[source] + product[source, 1, rows, :]
        core_copy(source).start()
        where = row_at(*SOURCES[source])
        result[core, pl.ds(pl.multiple_of(where * SHARE, SHARE), SHARE), :] = crossed[
            source, pl.ds(pl.multiple_of(core * SHARE, SHARE), SHARE), :
        ]

    for task in ORDER:
        if task[0] == "arrive":
            arrive(task[1], task[2])
        elif task[0] == "product":
            multiply(task[1], task[2])
        elif task[0] == "minus":
            pass_on(task[1], 1, 0, SUPER + SUPER // 2, "far_b", "minus_b")
        elif task[0] == "plus":
            pass_on(task[1], 0, 1, 0, "far_a", "plus_a")
        elif task[0] == "own":
            own(task[1])
        else:
            pair(task[1])

    def own_load(half):
        rows = pl.ds(pl.multiple_of(row * depth, SUPER), depth)
        return pltpu.make_async_copy(
            panel.at[rows, pl.ds(half * SUPER, SUPER)], chunk.at[half], chunk_sem.at[half]
        )

    own_load(0).start()
    own_load(1).start()
    own_load(0).wait()
    own_load(1).wait()

    def core_wait(step, carry):
        place = result.at[1 - core, pl.ds(pl.multiple_of(step * SHARE, SHARE), SHARE)]
        pltpu.make_async_copy(place, place, core_recv.at[step]).wait()
        return carry

    lax.fori_loop(0, ROWS, core_wait, 0)

    for half in range(2):
        total = jnp.zeros((SUPER, SUPER), jnp.float32)
        for block in range(blocks):
            keep = kept(row * blocks + block, col * 2 + half)
            lanes = slice(block * SUPER, (block + 1) * SUPER)
            side, first = (block * SUPER) // half_rows, (block * SUPER) % half_rows
            tile = result[side, half * SUPER:(half + 1) * SUPER, first:first + SUPER]
            off[half * SUPER:(half + 1) * SUPER, lanes] = tile * (-keep)
            t_high, t_low = split(tile)
            p_high, p_low = split(chunk[half, lanes, :] * keep)
            total += jnp.dot(t_high, p_low, preferred_element_type=jnp.float32)
            total += jnp.dot(t_low, p_high, preferred_element_type=jnp.float32)
            total += jnp.dot(t_high, p_high, preferred_element_type=jnp.float32)
        share = SUPER // ROWS
        for target in range(ROWS):
            mine[target, half] = total[target * share:(target + 1) * share]

    def diag_copy(step):
        target = lax.rem(row + step, ROWS)
        return remote(
            mine.at[target], theirs.at[step], diag_send.at[step], diag_recv.at[step], (target, col)
        )

    for step in range(1, ROWS):
        diag_copy(step).start()
    total = diag[...] + mine[row]
    for step in range(1, ROWS):
        diag_copy(step).wait_recv()
        total += theirs[step]
    diag_out[...] = total

    for step in range(1, ROWS):
        diag_copy(step).wait_send()
    for index in range(3):
        a_swap(index).wait_send()
    for message in range(len(HEAD)):
        if stays(message) is None:
            head_copy(message).wait_send()
        else:

            @pl.when(jnp.logical_not(stays(message)))
            def _():
                head_copy(message).wait_send()

    for source, half, way in SENDS:
        gather_copy(source, half, way).wait_send()
    for source in range(ROWS):
        for name in PARTS:
            part(source, name).wait_send()
        core_copy(source).wait_send()


def body(ancestor_inv, lower_panel, diag_block_inv, pattern):
    depth, width = ancestor_inv.shape
    width_here = lower_panel.shape[1]
    share = SUPER // ROWS
    half = SUPER // 2
    f32, bf16 = jnp.float32, jnp.bfloat16
    dma = pltpu.SemaphoreType.DMA
    return pl.pallas_call(
        kernel,
        out_shape=(
            jax.ShapeDtypeStruct((width_here, depth), f32),
            jax.ShapeDtypeStruct(diag_block_inv.shape, f32),
        ),
        in_specs=[
            pl.BlockSpec(memory_space=pltpu.SMEM),
            pl.BlockSpec(memory_space=pl.ANY),
            pl.BlockSpec(memory_space=pl.ANY),
            pl.BlockSpec(memory_space=pltpu.VMEM),
        ],
        out_specs=(pl.BlockSpec(memory_space=pltpu.VMEM), pl.BlockSpec(memory_space=pltpu.VMEM)),
        scratch_shapes=[
            pltpu.VMEM((ROWS, 2, 2, SUPER, depth), f32),
            pltpu.VMEM((depth, width), bf16),
            pltpu.VMEM((depth, width), bf16),
            pltpu.VMEM((2 * SUPER, depth), bf16),
            pltpu.VMEM((2 * SUPER, depth), bf16),
            pltpu.VMEM((ROWS, 2, 2 * SUPER, width), f32),
            pltpu.VMEM((ROWS, 2, half, width), f32),
            pltpu.VMEM((ROWS, 4, half, width), f32),
            pltpu.VMEM((ROWS, half, width), f32),
            pltpu.VMEM((2, width_here, width), f32),
            pltpu.VMEM((2, depth, SUPER), f32),
            pltpu.VMEM((SUPER, depth), f32),
            pltpu.VMEM((len(HEAD), SHARE, depth), f32),
            pltpu.VMEM((ROWS, 2, share, SUPER), f32),
            pltpu.VMEM((ROWS, 2, share, SUPER), f32),
            dma((2,)),
            dma((3,)),
            dma((3,)),
            dma((3,)),
            dma((len(HEAD),)),
            dma((2, 4)),
            dma((len(SENDS),)),
            dma((ROWS, 2, 2)),
            dma((ROWS, 7)),
            dma((ROWS, 7)),
            dma((ROWS,)),
            dma((ROWS,)),
            dma((ROWS,)),
            dma((ROWS,)),
        ],
        compiler_params=pltpu.CompilerParams(
            collective_id=0, has_side_effects=True, vmem_limit_bytes=63 * 2**20
        ),
        cost_estimate=pl.CostEstimate(
            flops=6 * depth * width * 16 * 2 * SUPER, bytes_accessed=16 * 2**20, transcendentals=0
        ),
    )(pattern, lower_panel, ancestor_inv, diag_block_inv)


def solution(mesh):
    in_specs = (P("row", "col"), P(None, "col"), P("col", "row", None), P())
    out_specs = (P("col", "row"), P("col", "row", None))
    return jax.shard_map(body, mesh=mesh, in_specs=in_specs, out_specs=out_specs, check_vma=False)
```

```python
import jax
import jax.numpy as jnp
from jax import lax
from jax.experimental import pallas as pl
from jax.experimental.pallas import tpu as pltpu
from jax.sharding import PartitionSpec as P

SUPER = 128
MESH = pl.DeviceIdType.MESH
RING = 4
ROWS = 8
SHARE = 32

SOURCES = ((0, 0), (0, 1), (-1, 0), (1, 0), (-1, 1), (1, 1), (2, 0), (2, 1))
HEAD = tuple((dx, dy, place) for dx, place in ((2, (0, 0)), (0, (1, 0)), (1, (0, 1)), (-1, (1, 1))) for dy in range(2))


def forwards(source, half):
    dz, dy = SOURCES[source]
    out = []
    if dz == 0:
        if dy == 0:
            out.append(("yh", SOURCES.index((0, 1))))
        out.append(("z+", SOURCES.index((-1, dy))))
        out.append(("z-", SOURCES.index((1, dy))))
    if dz == -1 and half == 0:
        out.append(("z+", SOURCES.index((2, dy))))
    if dz == 1 and half == 1:
        out.append(("z-", SOURCES.index((2, dy))))
    out.append(("core", source))
    return out


SENDS = {}
for _source in range(ROWS):
    for _half in range(2):
        for _way, _ in forwards(_source, _half):
            SENDS[(_source, _half, _way)] = len(SENDS)

ORDER = (
    ("convert", 0),
    ("arrive", 0, 0),
    ("convert", 1),
    ("arrive", 0, 1),
    ("product", 0, 0),
    ("product", 0, 1),
    ("minus", 0, 0),
    ("plus", 0, 0),
    ("arrive", 2, 0),
    ("arrive", 3, 0),
    ("arrive", 1, 0),
    ("own", 0, 0),
    ("product", 2, 0),
    ("product", 3, 0),
    ("product", 1, 0),
    ("pair", 0, 0),
    ("arrive", 2, 1),
    ("arrive", 3, 1),
    ("arrive", 1, 1),
    ("product", 2, 1),
    ("minus", 2, 0),
    ("plus", 2, 0),
    ("product", 3, 1),
    ("minus", 3, 0),
    ("plus", 3, 0),
    ("product", 1, 1),
    ("minus", 1, 0),
    ("plus", 1, 0),
    ("arrive", 5, 0),
    ("arrive", 6, 0),
    ("own", 2, 0),
    ("product", 5, 0),
    ("product", 6, 0),
    ("own", 3, 0),
    ("pair", 2, 0),
    ("first", 5, 0),
    ("arrive", 4, 0),
    ("arrive", 6, 1),
    ("first", 5, 1),
    ("own", 1, 0),
    ("product", 4, 0),
    ("pair", 3, 0),
    ("product", 6, 1),
    ("minus", 6, 0),
    ("plus", 6, 0),
    ("pair", 1, 0),
    ("first", 4, 0),
    ("arrive", 4, 1),
    ("arrive", 5, 1),
    ("first", 4, 1),
    ("product", 4, 1),
    ("own", 6, 0),
    ("product", 5, 1),
    ("first", 4, 2),
    ("minus", 4, 0),
    ("arrive", 7, 0),
    ("first", 4, 3),
    ("arrive", 7, 1),
    ("plus", 4, 0),
    ("product", 7, 0),
    ("pair", 6, 0),
    ("product", 7, 1),
    ("minus", 7, 0),
    ("plus", 7, 0),
    ("own", 4, 0),
    ("minus", 7, 1),
    ("plus", 7, 1),
    ("first", 5, 2),
    ("minus", 5, 0),
    ("minus", 7, 2),
    ("plus", 7, 2),
    ("first", 5, 3),
    ("plus", 5, 0),
    ("own", 7, 0),
    ("own", 7, 1),
    ("pair", 7, 0),
    ("pair", 7, 1),
    ("own", 7, 2),
    ("own", 5, 0),
    ("pair", 7, 2),
)
TILES = (1, 1, 1, 1, 1, 1, 1, 3)
PAIR_FIRST = (4, 5)
PARTS = ("far_a", "far_b", "minus_a", "plus_b", "minus_b", "plus_a", "cross")


def split(value):
    high = value.astype(jnp.bfloat16)
    low = (value - high.astype(jnp.float32)).astype(jnp.bfloat16)
    return high, low


def kernel(
    pattern, panel, ancestor, diag, off, diag_out,
    gathered, a_high, a_low, m_high, m_low, product, far, near, crossed, paired, result, chunk, turned, pieces, mine, theirs,
    chunk_sem, a_sem, a_send, a_recv, head_send, head_recv, gather_send, gather_recv, part_send, part_recv, pair_send, pair_recv,
    core_send, core_recv, diag_send, diag_recv,
):
    row, col = lax.axis_index("row"), lax.axis_index("col")
    y_hi, z = row // RING, lax.rem(row, RING)
    x, y_lo, core = col // 4, lax.rem(col // 2, 2), lax.rem(col, 2)
    rows_here, cols_here = ancestor.shape
    depth = rows_here
    blocks = depth // SUPER
    half_rows = rows_here // 2

    def col_at(dx, dy, target_core):
        nx = lax.rem(x + (dx + RING), RING)
        ny = 1 - y_lo if dy else y_lo
        return nx * 4 + ny * 2 + target_core

    def row_at(dz, dy):
        nz = lax.rem(z + (dz + RING), RING)
        return (1 - y_hi if dy else y_hi) * RING + nz

    ways = {
        "x+": (row, col_at(1, 0, core)),
        "x-": (row, col_at(-1, 0, core)),
        "y": (row, col_at(0, 1, core)),
        "core": (row, col_at(0, 0, 1 - core)),
        "z+": (row_at(1, 0), col),
        "z-": (row_at(-1, 0), col),
        "yh": (row_at(0, 1), col),
    }

    def remote(source, target, send, recv, device):
        return pltpu.make_async_remote_copy(
            src_ref=source, dst_ref=target, send_sem=send, recv_sem=recv, device_id=device, device_id_type=MESH
        )

    barrier = pltpu.get_barrier_semaphore()

    def greet(device):
        pl.semaphore_signal(barrier, inc=1, device_id=device, device_id_type=MESH)

    def greet_row(step, carry):
        greet((row, lax.rem(col + step, 16)))
        return carry

    lax.fori_loop(1, 16, greet_row, 0)
    for way in ("z+", "z-", "yh"):
        greet(ways[way])

    def chunk_load(message):
        dx, dy, _ = HEAD[message]
        chip = col_at(dx, dy, 0) // 2
        rows = pl.ds(pl.multiple_of(chip * depth, SUPER), depth)
        lanes = pl.ds(pl.multiple_of((row // 4) * SUPER, SUPER), SUPER)
        return pltpu.make_async_copy(panel.at[rows, lanes], chunk.at[message % 2], chunk_sem.at[message % 2])

    def a_rows(which, part):
        return ancestor.at[pl.ds(pl.multiple_of(which * half_rows + part * 256, 256), 256)]

    own_place = ((2, 0), (2, 1), (3, 0))
    other_place = ((3, 1), (4, 0), (4, 1))

    def a_load(part):
        slot, half = own_place[part]
        return pltpu.make_async_copy(a_rows(core, part), product.at[slot, half], a_sem.at[part])

    def a_swap(part):
        slot, half = other_place[part]
        return remote(
            a_rows(1 - core, part), product.at[slot, half], a_send.at[part], a_recv.at[part], ways["core"]
        )

    chunk_load(0).start()
    chunk_load(1).start()
    for part in range(3):
        a_load(part).start()

    def kept(block_row, column):
        return pattern[block_row, column].astype(jnp.float32)

    def head_copy(message):
        dx, dy, (target_core, half) = HEAD[message]
        piece = y_lo * 2 + core
        return remote(
            pieces.at[message],
            gathered.at[0, target_core, half, pl.ds(pl.multiple_of(piece * SHARE, SHARE), SHARE)],
            head_send.at[message],
            head_recv.at[half, piece],
            (row, col_at(dx, dy, target_core)),
        )

    def head_stay(message):
        _, _, (target_core, half) = HEAD[message]
        piece = y_lo * 2 + core
        return pltpu.make_async_copy(
            pieces.at[message],
            gathered.at[0, target_core, half, pl.ds(pl.multiple_of(piece * SHARE, SHARE), SHARE)],
            head_recv.at[half, piece],
        )

    def stays(message):
        dx, dy, (target_core, _) = HEAD[message]
        return core == target_core if (dx, dy) == (0, 0) else None

    def turn(message):
        dx, dy, _ = HEAD[message]
        chip = col_at(dx, dy, 0) // 2
        chunk_load(message).wait()

        def block_turn(block, carry):
            rows = pl.ds(pl.multiple_of(block * SUPER, SUPER), SUPER)
            tile = chunk[message % 2, rows, :] * kept(chip * blocks + block, col * 2 + row // 4)
            turned[:, rows] = tile.T
            return carry

        lax.fori_loop(0, blocks, block_turn, 0, unroll=2)
        if message + 2 < len(HEAD):
            chunk_load(message + 2).start()
        pieces[message] = turned[pl.ds(pl.multiple_of(lax.rem(row, 4) * SHARE, SHARE), SHARE), :]

    turn(0)
    pl.semaphore_wait(barrier, 18)
    for part in range(3):
        a_swap(part).start()
    for message in range(len(HEAD)):
        if message > 0:
            turn(message)
        if stays(message) is None:
            head_copy(message).start()
        else:

            @pl.when(stays(message))
            def _():
                head_stay(message).start()

            @pl.when(jnp.logical_not(stays(message)))
            def _():
                head_copy(message).start()

    def own_load(half):
        rows = pl.ds(pl.multiple_of(row * depth, SUPER), depth)
        return pltpu.make_async_copy(
            panel.at[rows, pl.ds(half * SUPER, SUPER)], chunk.at[half], chunk_sem.at[half]
        )

    own_load(0).start()
    own_load(1).start()

    def convert(place, part, offset):
        slot, half = place[part]
        for step in range(2):
            for side in range(cols_here // 256):
                tile = product[slot, half, step * SUPER:(step + 1) * SUPER, side * 256:(side + 1) * 256].T
                high, low = split(tile)
                rows = pl.ds(pl.multiple_of(offset + side * 256, 256), 256)
                lanes = slice(part * 256 + step * SUPER, part * 256 + (step + 1) * SUPER)
                a_high[rows, lanes] = high
                a_low[rows, lanes] = low

    def convert_all(swapped):
        for part in range(3):
            if swapped:
                a_swap(part).wait_recv()
                convert(other_place, part, (1 - core) * cols_here)
            else:
                a_load(part).wait()
                convert(own_place, part, core * cols_here)

    def gather_copy(source, half, way, rows=slice(None)):
        target = dict(forwards(source, half))[way]
        return remote(
            gathered.at[source, core, half, rows],
            gathered.at[target, core, half, rows],
            gather_send.at[SENDS[(source, half, way)]],
            gather_recv.at[target, core, half],
            ways[way],
        )

    def landed(source, which, half):
        place = gathered.at[source, which, half]
        pltpu.make_async_copy(place, place, gather_recv.at[source, which, half]).wait()

    def arrive(source, half):
        if source > 0:
            landed(source, core, half)
            for way, _ in forwards(source, half):
                gather_copy(source, half, way).start()
            return
        for step in range(4):
            piece = ((1 - y_lo) if step >= 2 else y_lo) * 2 + step % 2
            rows = pl.ds(pl.multiple_of(piece * SHARE, SHARE), SHARE)
            place = gathered.at[0, core, half, rows]
            pltpu.make_async_copy(place, place, head_recv.at[half, piece]).wait()
            for way, _ in forwards(source, half):
                gather_copy(source, half, way, rows).start()

    def tiles(source):
        count = TILES[source]
        return [slice(t * half_rows // count, (t + 1) * half_rows // count) for t in range(count)]

    def part(source, name, tile=None):
        lanes = slice(None) if tile is None else tiles(source)[tile]
        index = PARTS.index(name)
        half = SUPER // 2
        if source in PAIR_FIRST:
            count = half // 2
            held = paired.at[PAIR_FIRST.index(source)]
            block, target, way = {
                "far_a": lambda: (held.at[0, pl.ds(0, count)], far.at[source, 0, pl.ds(0, count)], "x+"),
                "far_b": lambda: (held.at[0, pl.ds(count, count)], far.at[source, 1, pl.ds(0, count)], "x-"),
                "minus_a": lambda: (held.at[2, pl.ds(0, count)], near.at[source, 0, pl.ds(0, count)], "x-"),
                "plus_b": lambda: (held.at[3, pl.ds(count, count)], near.at[source, 1, pl.ds(0, count)], "x+"),
                "minus_b": lambda: (far.at[source, 1, pl.ds(0, count)], near.at[source, 2, pl.ds(0, count)], "x-"),
                "plus_a": lambda: (far.at[source, 0, pl.ds(0, count)], near.at[source, 3, pl.ds(0, count)], "x+"),
            }[name]()
            return remote(
                block, target, part_send.at[source, index], part_recv.at[source, index, 0], ways[way]
            )
        first, second = product.at[source, 0], product.at[source, 1]
        block, target, way = {
            "far_a": lambda: (first.at[pl.ds(0, half), lanes], far.at[source, 0, :, lanes], "x+"),
            "far_b": lambda: (first.at[pl.ds(half, half), lanes], far.at[source, 1, :, lanes], "x-"),
            "minus_a": lambda: (second.at[pl.ds(0, half), lanes], near.at[source, 0, :, lanes], "x-"),
            "plus_b": lambda: (second.at[pl.ds(3 * half, half), lanes], near.at[source, 1, :, lanes], "x+"),
            "minus_b": lambda: (far.at[source, 1, :, lanes], near.at[source, 2, :, lanes], "x-"),
            "plus_a": lambda: (far.at[source, 0, :, lanes], near.at[source, 3, :, lanes], "x+"),
            "cross": lambda: (
                first.at[pl.ds(pl.multiple_of(2 * half + (1 - y_lo) * half, half), half), lanes],
                crossed.at[source, :, lanes],
                "y",
            ),
        }[name]()
        return remote(
            block, target, part_send.at[source, index], part_recv.at[source, index, tile or 0], ways[way]
        )

    def pair_copy(source, unit):
        half = SUPER // 2
        rows = pl.ds(pl.multiple_of((unit % 2) * SUPER + (1 - y_lo) * half, half), half)
        place = PAIR_FIRST.index(source)
        return remote(
            product.at[source, unit // 2, rows],
            paired.at[place, unit],
            pair_send.at[place, unit],
            pair_recv.at[place, unit],
            ways["y"],
        )

    def pair_first(source, unit):
        pair_copy(source, unit).wait_recv()
        half = SUPER // 2
        rows = pl.ds(pl.multiple_of((unit % 2) * SUPER + y_lo * half, half), half)
        place = PAIR_FIRST.index(source)
        paired[place, unit] = paired[place, unit] + product[source, unit // 2, rows, :]
        for name in (("far_a", "far_b"), (), ("minus_a",), ("plus_b",))[unit]:
            part(source, name, 0).start()

    def multiply(source, half):
        landed(source, 1 - core, half)
        for which in range(2):
            def prepare(step, carry):
                rows = pl.ds(pl.multiple_of(step * 32, 32), 32)
                out = pl.ds(pl.multiple_of(which * SUPER + step * 32, 32), 32)
                high, low = split(gathered[source, which, half, rows, :])
                m_high[out, :] = high
                m_low[out, :] = low
                return carry

            lax.fori_loop(0, SUPER // 32, prepare, 0)

        def tile(step, carry):
            lanes = pl.ds(pl.multiple_of(step * 256, 256), 256)
            high = a_high[:, lanes]
            total = jnp.dot(m_low[...], high, preferred_element_type=jnp.float32)
            total += jnp.dot(m_high[...], a_low[:, lanes], preferred_element_type=jnp.float32)
            total += jnp.dot(m_high[...], high, preferred_element_type=jnp.float32)
            product[source, half, :, lanes] = total
            return carry

        lax.fori_loop(0, half_rows // 256, tile, 0)
        if source in PAIR_FIRST:
            for unit in (2 * half, 2 * half + 1):
                pair_copy(source, unit).start()
            return
        for index in range(TILES[source]):
            for name in ("far_a", "far_b") if half == 0 else ("minus_a", "plus_b"):
                part(source, name, index).start()

    def pass_on(source, tile, which, first, arriving, leaving):
        part(source, arriving, tile).wait_recv()
        count = SUPER // 2
        lanes = tiles(source)[tile]
        if source in PAIR_FIRST:
            count = count // 2
            unit, start = ((3, 0), (2, count))[which]
            far[source, which, :count] = far[source, which, :count] + paired[
                PAIR_FIRST.index(source), unit, start:start + count
            ]
            part(source, leaving, tile).start()
            return
        far[source, which, :, lanes] = far[source, which, :, lanes] + product[source, 1, first:first + count, lanes]
        part(source, leaving, tile).start()

    def own(source, tile):
        count = SUPER // 2
        lanes = tiles(source)[tile]
        for name in ("minus_a", "plus_b", "minus_b", "plus_a"):
            part(source, name, tile).wait_recv()
        if source in PAIR_FIRST:
            count = count // 2
            place = PAIR_FIRST.index(source)
            for first, one, two in ((0, 0, 3), (count, 1, 2)):
                crossed[source, first:first + count] = (
                    paired[place, 1, first:first + count] + near[source, one, :count] + near[source, two, :count]
                )
            hand_over(source, lanes)
            return
        for first, one, two in ((2 * count, 0, 3), (3 * count, 1, 2)):
            product[source, 0, first:first + count, lanes] = (
                product[source, 0, first:first + count, lanes] + near[source, one, :, lanes] + near[source, two, :, lanes]
            )
        part(source, "cross", tile).start()

    def core_copy(source, lanes=slice(None)):
        where = row_at(*SOURCES[source])
        return remote(
            crossed.at[source, pl.ds(pl.multiple_of((1 - core) * SHARE, SHARE), SHARE), lanes],
            result.at[core, pl.ds(pl.multiple_of(where * SHARE, SHARE), SHARE), lanes],
            core_send.at[source],
            core_recv.at[where],
            ways["core"],
        )

    def pair(source, tile):
        part(source, "cross", tile).wait_recv()
        lanes = tiles(source)[tile]
        half = SUPER // 2
        rows = pl.ds(pl.multiple_of(2 * half + y_lo * half, half), half)
        crossed[source, :, lanes] = crossed[source, :, lanes] + product[source, 0, rows, lanes]
        hand_over(source, lanes)

    def hand_over(source, lanes):
        core_copy(source, lanes).start()
        where = row_at(*SOURCES[source])
        result[core, pl.ds(pl.multiple_of(where * SHARE, SHARE), SHARE), lanes] = crossed[
            source, pl.ds(pl.multiple_of(core * SHARE, SHARE), SHARE), lanes
        ]

    for task in ORDER:
        if task[0] == "arrive":
            arrive(task[1], task[2])
        elif task[0] == "convert":
            convert_all(task[1] == 1)
        elif task[0] == "product":
            multiply(task[1], task[2])
        elif task[0] == "minus":
            pass_on(task[1], task[2], 1, SUPER // 2, "far_b", "minus_b")
        elif task[0] == "plus":
            pass_on(task[1], task[2], 0, SUPER, "far_a", "plus_a")
        elif task[0] == "first":
            pair_first(task[1], task[2])
        elif task[0] == "own":
            own(task[1], task[2])
        else:
            pair(task[1], task[2])

    own_load(0).wait()
    own_load(1).wait()

    def core_wait(step, carry):
        place = result.at[1 - core, pl.ds(pl.multiple_of(step * SHARE, SHARE), SHARE)]
        pltpu.make_async_copy(place, place, core_recv.at[step]).wait()
        return carry

    lax.fori_loop(0, ROWS, core_wait, 0)

    def tile_of(half, block):
        side, first = (block * SUPER) // half_rows, (block * SUPER) % half_rows
        return result[side, half * SUPER:(half + 1) * SUPER, first:first + SUPER]

    for half in range(2):
        total = jnp.zeros((SUPER, SUPER), jnp.float32)
        for block in range(blocks):
            lanes = slice(block * SUPER, (block + 1) * SUPER)
            t_high, t_low = split(tile_of(half, block))
            p_high, p_low = split(chunk[half, lanes, :] * kept(row * blocks + block, col * 2 + half))
            total += jnp.dot(t_high, p_low, preferred_element_type=jnp.float32)
            total += jnp.dot(t_low, p_high, preferred_element_type=jnp.float32)
            total += jnp.dot(t_high, p_high, preferred_element_type=jnp.float32)
        share = SUPER // ROWS
        for target in range(ROWS):
            mine[target, half] = total[target * share:(target + 1) * share]

    def diag_copy(step):
        target = lax.rem(row + step, ROWS)
        return remote(
            mine.at[target], theirs.at[step], diag_send.at[step], diag_recv.at[step], (target, col)
        )

    for step in range(1, ROWS):
        diag_copy(step).start()

    for half in range(2):
        for block in range(blocks):
            keep = kept(row * blocks + block, col * 2 + half)
            off[half * SUPER:(half + 1) * SUPER, block * SUPER:(block + 1) * SUPER] = tile_of(half, block) * (-keep)
    for index in range(3):
        a_swap(index).wait_send()
    for message in range(len(HEAD)):
        if stays(message) is None:
            head_copy(message).wait_send()
        else:

            @pl.when(jnp.logical_not(stays(message)))
            def _():
                head_copy(message).wait_send()

    for source, half, way in SENDS:
        gather_copy(source, half, way).wait_send()
    for source in range(ROWS):
        for name in PARTS[:6] if source in PAIR_FIRST else PARTS:
            part(source, name).wait_send()
        if source in PAIR_FIRST:
            for unit in range(4):
                pair_copy(source, unit).wait_send()
        core_copy(source).wait_send()

    total = diag[...] + mine[row]
    for step in range(1, ROWS):
        diag_copy(step).wait_recv()
        total += theirs[step]
    diag_out[...] = total
    for step in range(1, ROWS):
        diag_copy(step).wait_send()


def body(ancestor_inv, lower_panel, diag_block_inv, pattern):
    depth, width = ancestor_inv.shape
    width_here = lower_panel.shape[1]
    share = SUPER // ROWS
    half = SUPER // 2
    f32, bf16 = jnp.float32, jnp.bfloat16
    dma = pltpu.SemaphoreType.DMA
    return pl.pallas_call(
        kernel,
        out_shape=(
            jax.ShapeDtypeStruct((width_here, depth), f32),
            jax.ShapeDtypeStruct(diag_block_inv.shape, f32),
        ),
        in_specs=[
            pl.BlockSpec(memory_space=pltpu.SMEM),
            pl.BlockSpec(memory_space=pl.ANY),
            pl.BlockSpec(memory_space=pl.ANY),
            pl.BlockSpec(memory_space=pltpu.VMEM),
        ],
        out_specs=(pl.BlockSpec(memory_space=pltpu.VMEM), pl.BlockSpec(memory_space=pltpu.VMEM)),
        scratch_shapes=[
            pltpu.VMEM((ROWS, 2, 2, SUPER, depth), f32),
            pltpu.VMEM((depth, width), bf16),
            pltpu.VMEM((depth, width), bf16),
            pltpu.VMEM((2 * SUPER, depth), bf16),
            pltpu.VMEM((2 * SUPER, depth), bf16),
            pltpu.VMEM((ROWS, 2, 2 * SUPER, width), f32),
            pltpu.VMEM((ROWS, 2, half, width), f32),
            pltpu.VMEM((ROWS, 4, half, width), f32),
            pltpu.VMEM((ROWS, half, width), f32),
            pltpu.VMEM((len(PAIR_FIRST), 4, half, width), f32),
            pltpu.VMEM((2, width_here, width), f32),
            pltpu.VMEM((2, depth, SUPER), f32),
            pltpu.VMEM((SUPER, depth), f32),
            pltpu.VMEM((len(HEAD), SHARE, depth), f32),
            pltpu.VMEM((ROWS, 2, share, SUPER), f32),
            pltpu.VMEM((ROWS, 2, share, SUPER), f32),
            dma((2,)),
            dma((3,)),
            dma((3,)),
            dma((3,)),
            dma((len(HEAD),)),
            dma((2, 4)),
            dma((len(SENDS),)),
            dma((ROWS, 2, 2)),
            dma((ROWS, 7)),
            dma((ROWS, 7, 3)),
            dma((len(PAIR_FIRST), 4)),
            dma((len(PAIR_FIRST), 4)),
            dma((ROWS,)),
            dma((ROWS,)),
            dma((ROWS,)),
            dma((ROWS,)),
        ],
        compiler_params=pltpu.CompilerParams(
            collective_id=0, has_side_effects=True, vmem_limit_bytes=63 * 2**20
        ),
        cost_estimate=pl.CostEstimate(
            flops=6 * depth * width * 16 * 2 * SUPER, bytes_accessed=16 * 2**20, transcendentals=0
        ),
    )(pattern, lower_panel, ancestor_inv, diag_block_inv)


def solution(mesh):
    in_specs = (P("row", "col"), P(None, "col"), P("col", "row", None), P())
    out_specs = (P("col", "row"), P("col", "row", None))
    return jax.shard_map(body, mesh=mesh, in_specs=in_specs, out_specs=out_specs, check_vma=False)
```

```python
import jax
import jax.numpy as jnp
from jax import lax
from jax.experimental import pallas as pl
from jax.experimental.pallas import tpu as pltpu
from jax.sharding import PartitionSpec as P

SUPER = 128
MESH = pl.DeviceIdType.MESH
RING = 4
ROWS = 8
SHARE = 32

SOURCES = ((0, 0), (0, 1), (-1, 0), (1, 0), (-1, 1), (1, 1), (2, 0), (2, 1))
HEAD = tuple((dx, dy, place) for dx, place in ((2, (0, 0)), (0, (1, 0)), (1, (0, 1)), (-1, (1, 1))) for dy in range(2))


def forwards(source, half):
    dz, dy = SOURCES[source]
    out = []
    if dz == 0:
        if dy == 0:
            out.append(("yh", SOURCES.index((0, 1))))
        out.append(("z+", SOURCES.index((-1, dy))))
        out.append(("z-", SOURCES.index((1, dy))))
    if dz == -1 and half == 0:
        out.append(("z+", SOURCES.index((2, dy))))
    if dz == 1 and half == 1:
        out.append(("z-", SOURCES.index((2, dy))))
    out.append(("core", source))
    return out


SENDS = {}
for _source in range(ROWS):
    for _half in range(2):
        for _way, _ in forwards(_source, _half):
            SENDS[(_source, _half, _way)] = len(SENDS)

ORDER = (
    ("convert", 0),
    ("rest", 1),
    ("convert", 1),
    ("product", 0, 0),
    ("product", 0, 1),
    ("minus", 0, 0),
    ("plus", 0, 0),
    ("arrive", 2, 0),
    ("arrive", 3, 0),
    ("arrive", 1, 0),
    ("own", 0, 0),
    ("product", 2, 0),
    ("product", 3, 0),
    ("product", 1, 0),
    ("pair", 0, 0),
    ("arrive", 2, 1),
    ("arrive", 3, 1),
    ("arrive", 1, 1),
    ("product", 2, 1),
    ("minus", 2, 0),
    ("plus", 2, 0),
    ("product", 3, 1),
    ("minus", 3, 0),
    ("plus", 3, 0),
    ("product", 1, 1),
    ("minus", 1, 0),
    ("plus", 1, 0),
    ("arrive", 5, 0),
    ("arrive", 6, 0),
    ("own", 2, 0),
    ("product", 5, 0),
    ("product", 6, 0),
    ("own", 3, 0),
    ("pair", 2, 0),
    ("first", 5, 0),
    ("arrive", 4, 0),
    ("arrive", 6, 1),
    ("first", 5, 1),
    ("own", 1, 0),
    ("product", 4, 0),
    ("pair", 3, 0),
    ("product", 6, 1),
    ("minus", 6, 0),
    ("plus", 6, 0),
    ("pair", 1, 0),
    ("first", 4, 0),
    ("arrive", 4, 1),
    ("arrive", 5, 1),
    ("first", 4, 1),
    ("product", 4, 1),
    ("own", 6, 0),
    ("product", 5, 1),
    ("first", 4, 2),
    ("minus", 4, 0),
    ("arrive", 7, 0),
    ("first", 4, 3),
    ("arrive", 7, 1),
    ("plus", 4, 0),
    ("product", 7, 0),
    ("pair", 6, 0),
    ("product", 7, 1),
    ("minus", 7, 0),
    ("plus", 7, 0),
    ("own", 4, 0),
    ("minus", 7, 1),
    ("plus", 7, 1),
    ("first", 5, 2),
    ("minus", 5, 0),
    ("minus", 7, 2),
    ("plus", 7, 2),
    ("first", 5, 3),
    ("plus", 5, 0),
    ("own", 7, 0),
    ("own", 7, 1),
    ("pair", 7, 0),
    ("pair", 7, 1),
    ("own", 7, 2),
    ("own", 5, 0),
    ("pair", 7, 2),
)
TILES = (1, 1, 1, 1, 1, 1, 1, 3)
PAIR_FIRST = (4, 5)
PARTS = ("far_a", "far_b", "minus_a", "plus_b", "minus_b", "plus_a", "cross")


def split(value):
    high = value.astype(jnp.bfloat16)
    low = (value - high.astype(jnp.float32)).astype(jnp.bfloat16)
    return high, low


def kernel(
    pattern_in, panel, ancestor, diag, off, diag_out,
    pattern,
    gathered, a_high, a_low, m_high, m_low, product, far, near, crossed, paired, result, chunk, turned, pieces, mine, theirs,
    chunk_sem, a_sem, a_send, a_recv, head_send, head_recv, gather_send, gather_recv, part_send, part_recv, pair_send, pair_recv,
    core_send, core_recv, diag_send, diag_recv, pattern_sem,
):
    row, col = lax.axis_index("row"), lax.axis_index("col")
    y_hi, z = row // RING, lax.rem(row, RING)
    x, y_lo, core = col // 4, lax.rem(col // 2, 2), lax.rem(col, 2)
    rows_here, cols_here = ancestor.shape
    depth = rows_here
    blocks = depth // SUPER
    half_rows = rows_here // 2

    def col_at(dx, dy, target_core):
        nx = lax.rem(x + (dx + RING), RING)
        ny = 1 - y_lo if dy else y_lo
        return nx * 4 + ny * 2 + target_core

    def row_at(dz, dy):
        nz = lax.rem(z + (dz + RING), RING)
        return (1 - y_hi if dy else y_hi) * RING + nz

    ways = {
        "x+": (row, col_at(1, 0, core)),
        "x-": (row, col_at(-1, 0, core)),
        "y": (row, col_at(0, 1, core)),
        "core": (row, col_at(0, 0, 1 - core)),
        "z+": (row_at(1, 0), col),
        "z-": (row_at(-1, 0), col),
        "yh": (row_at(0, 1), col),
    }

    def remote(source, target, send, recv, device):
        return pltpu.make_async_remote_copy(
            src_ref=source, dst_ref=target, send_sem=send, recv_sem=recv, device_id=device, device_id_type=MESH
        )

    pattern_copy = pltpu.make_async_copy(pattern_in, pattern, pattern_sem)
    pattern_copy.start()

    barrier = pltpu.get_barrier_semaphore()

    def greet(device):
        pl.semaphore_signal(barrier, inc=1, device_id=device, device_id_type=MESH)

    def greet_row(step, carry):
        greet((row, lax.rem(col + step, 16)))
        return carry

    lax.fori_loop(1, 16, greet_row, 0)
    for way in ("z+", "z-", "yh"):
        greet(ways[way])

    def chunk_load(message):
        dx, dy, _ = HEAD[message]
        chip = col_at(dx, dy, 0) // 2
        rows = pl.ds(pl.multiple_of(chip * depth, SUPER), depth)
        lanes = pl.ds(pl.multiple_of((row // 4) * SUPER, SUPER), SUPER)
        return pltpu.make_async_copy(panel.at[rows, lanes], chunk.at[message % 2], chunk_sem.at[message % 2])

    def a_rows(which, part):
        return ancestor.at[pl.ds(pl.multiple_of(which * half_rows + part * 256, 256), 256)]

    own_place = ((2, 0), (2, 1), (3, 0))
    other_place = ((3, 1), (4, 0), (4, 1))

    def a_load(part):
        slot, half = own_place[part]
        return pltpu.make_async_copy(a_rows(core, part), product.at[slot, half], a_sem.at[part])

    def a_swap(part):
        slot, half = other_place[part]
        return remote(
            a_rows(1 - core, part), product.at[slot, half], a_send.at[part], a_recv.at[part], ways["core"]
        )

    chunk_load(0).start()
    chunk_load(1).start()
    for part in range(3):
        a_load(part).start()

    def kept(block_row, column):
        return pattern[block_row, column].astype(jnp.float32)

    def head_copy(message):
        dx, dy, (target_core, half) = HEAD[message]
        piece = y_lo * 2 + core
        return remote(
            pieces.at[message],
            gathered.at[0, target_core, half, pl.ds(pl.multiple_of(piece * SHARE, SHARE), SHARE)],
            head_send.at[message],
            head_recv.at[half, piece],
            (row, col_at(dx, dy, target_core)),
        )

    def head_stay(message):
        _, _, (target_core, half) = HEAD[message]
        piece = y_lo * 2 + core
        return pltpu.make_async_copy(
            pieces.at[message],
            gathered.at[0, target_core, half, pl.ds(pl.multiple_of(piece * SHARE, SHARE), SHARE)],
            head_recv.at[half, piece],
        )

    def stays(message):
        dx, dy, (target_core, _) = HEAD[message]
        return core == target_core if (dx, dy) == (0, 0) else None

    def turn(message):
        dx, dy, _ = HEAD[message]
        chip = col_at(dx, dy, 0) // 2
        chunk_load(message).wait()

        def block_turn(block, carry):
            rows = pl.ds(pl.multiple_of(block * SUPER, SUPER), SUPER)
            tile = chunk[message % 2, rows, :] * kept(chip * blocks + block, col * 2 + row // 4)
            turned[:, rows] = tile.T
            return carry

        lax.fori_loop(0, blocks, block_turn, 0, unroll=2)
        if message + 2 < len(HEAD):
            chunk_load(message + 2).start()
        pieces[message] = turned[pl.ds(pl.multiple_of(lax.rem(row, 4) * SHARE, SHARE), SHARE), :]

    def gather_copy(source, half, way, rows=slice(None)):
        target = dict(forwards(source, half))[way]
        return remote(
            gathered.at[source, core, half, rows],
            gathered.at[target, core, half, rows],
            gather_send.at[SENDS[(source, half, way)]],
            gather_recv.at[target, core, half],
            ways[way],
        )

    def landed(source, which, half):
        place = gathered.at[source, which, half]
        pltpu.make_async_copy(place, place, gather_recv.at[source, which, half]).wait()

    def arrive(source, half):
        if source > 0:
            landed(source, core, half)
            for way, _ in forwards(source, half):
                gather_copy(source, half, way).start()
            return
        first_sends(half, (0, 1, 2, 3))

    def first_sends(half, steps):
        for step in steps:
            piece = ((1 - y_lo) if step >= 2 else y_lo) * 2 + step % 2
            rows = pl.ds(pl.multiple_of(piece * SHARE, SHARE), SHARE)
            place = gathered.at[0, core, half, rows]
            pltpu.make_async_copy(place, place, head_recv.at[half, piece]).wait()
            for way, _ in forwards(0, half):
                gather_copy(0, half, way, rows).start()

    pattern_copy.wait()
    turn(0)
    pl.semaphore_wait(barrier, 18)
    for part in range(3):
        a_swap(part).start()
    for message in range(len(HEAD)):
        if message > 0:
            turn(message)
        if stays(message) is None:
            head_copy(message).start()
        else:

            @pl.when(stays(message))
            def _():
                head_stay(message).start()

            @pl.when(jnp.logical_not(stays(message)))
            def _():
                head_copy(message).start()

        if message == 3:
            first_sends(0, (0, 1))
        if message == 7:
            first_sends(0, (2, 3))

    def own_load(half):
        rows = pl.ds(pl.multiple_of(row * depth, SUPER), depth)
        return pltpu.make_async_copy(
            panel.at[rows, pl.ds(half * SUPER, SUPER)], chunk.at[half], chunk_sem.at[half]
        )

    own_load(0).start()
    own_load(1).start()

    def convert(place, part, offset):
        slot, half = place[part]
        for step in range(2):
            for side in range(cols_here // 256):
                tile = product[slot, half, step * SUPER:(step + 1) * SUPER, side * 256:(side + 1) * 256].T
                high, low = split(tile)
                rows = pl.ds(pl.multiple_of(offset + side * 256, 256), 256)
                lanes = slice(part * 256 + step * SUPER, part * 256 + (step + 1) * SUPER)
                a_high[rows, lanes] = high
                a_low[rows, lanes] = low

    def convert_all(swapped):
        for part in range(3):
            if swapped:
                a_swap(part).wait_recv()
                convert(other_place, part, (1 - core) * cols_here)
            else:
                a_load(part).wait()
                convert(own_place, part, core * cols_here)

    def tiles(source):
        count = TILES[source]
        return [slice(t * half_rows // count, (t + 1) * half_rows // count) for t in range(count)]

    def part(source, name, tile=None):
        lanes = slice(None) if tile is None else tiles(source)[tile]
        index = PARTS.index(name)
        half = SUPER // 2
        if source in PAIR_FIRST:
            count = half // 2
            held = paired.at[PAIR_FIRST.index(source)]
            block, target, way = {
                "far_a": lambda: (held.at[0, pl.ds(0, count)], far.at[source, 0, pl.ds(0, count)], "x+"),
                "far_b": lambda: (held.at[0, pl.ds(count, count)], far.at[source, 1, pl.ds(0, count)], "x-"),
                "minus_a": lambda: (held.at[2, pl.ds(0, count)], near.at[source, 0, pl.ds(0, count)], "x-"),
                "plus_b": lambda: (held.at[3, pl.ds(count, count)], near.at[source, 1, pl.ds(0, count)], "x+"),
                "minus_b": lambda: (far.at[source, 1, pl.ds(0, count)], near.at[source, 2, pl.ds(0, count)], "x-"),
                "plus_a": lambda: (far.at[source, 0, pl.ds(0, count)], near.at[source, 3, pl.ds(0, count)], "x+"),
            }[name]()
            return remote(
                block, target, part_send.at[source, index], part_recv.at[source, index, 0], ways[way]
            )
        first, second = product.at[source, 0], product.at[source, 1]
        block, target, way = {
            "far_a": lambda: (first.at[pl.ds(0, half), lanes], far.at[source, 0, :, lanes], "x+"),
            "far_b": lambda: (first.at[pl.ds(half, half), lanes], far.at[source, 1, :, lanes], "x-"),
            "minus_a": lambda: (second.at[pl.ds(0, half), lanes], near.at[source, 0, :, lanes], "x-"),
            "plus_b": lambda: (second.at[pl.ds(3 * half, half), lanes], near.at[source, 1, :, lanes], "x+"),
            "minus_b": lambda: (far.at[source, 1, :, lanes], near.at[source, 2, :, lanes], "x-"),
            "plus_a": lambda: (far.at[source, 0, :, lanes], near.at[source, 3, :, lanes], "x+"),
            "cross": lambda: (
                first.at[pl.ds(pl.multiple_of(2 * half + (1 - y_lo) * half, half), half), lanes],
                crossed.at[source, :, lanes],
                "y",
            ),
        }[name]()
        return remote(
            block, target, part_send.at[source, index], part_recv.at[source, index, tile or 0], ways[way]
        )

    def pair_copy(source, unit):
        half = SUPER // 2
        rows = pl.ds(pl.multiple_of((unit % 2) * SUPER + (1 - y_lo) * half, half), half)
        place = PAIR_FIRST.index(source)
        return remote(
            product.at[source, unit // 2, rows],
            paired.at[place, unit],
            pair_send.at[place, unit],
            pair_recv.at[place, unit],
            ways["y"],
        )

    def pair_first(source, unit):
        pair_copy(source, unit).wait_recv()
        half = SUPER // 2
        rows = pl.ds(pl.multiple_of((unit % 2) * SUPER + y_lo * half, half), half)
        place = PAIR_FIRST.index(source)
        paired[place, unit] = paired[place, unit] + product[source, unit // 2, rows, :]
        for name in (("far_a", "far_b"), (), ("minus_a",), ("plus_b",))[unit]:
            part(source, name, 0).start()

    def multiply(source, half):
        landed(source, 1 - core, half)
        for which in range(2):
            def prepare(step, carry):
                rows = pl.ds(pl.multiple_of(step * 32, 32), 32)
                out = pl.ds(pl.multiple_of(which * SUPER + step * 32, 32), 32)
                high, low = split(gathered[source, which, half, rows, :])
                m_high[out, :] = high
                m_low[out, :] = low
                return carry

            lax.fori_loop(0, SUPER // 32, prepare, 0)

        def tile(step, carry):
            lanes = pl.ds(pl.multiple_of(step * 256, 256), 256)
            high = a_high[:, lanes]
            total = jnp.dot(m_low[...], high, preferred_element_type=jnp.float32)
            total += jnp.dot(m_high[...], a_low[:, lanes], preferred_element_type=jnp.float32)
            total += jnp.dot(m_high[...], high, preferred_element_type=jnp.float32)
            product[source, half, :, lanes] = total
            return carry

        lax.fori_loop(0, half_rows // 256, tile, 0)
        if source in PAIR_FIRST:
            for unit in (2 * half, 2 * half + 1):
                pair_copy(source, unit).start()
            return
        for index in range(TILES[source]):
            for name in ("far_a", "far_b") if half == 0 else ("minus_a", "plus_b"):
                part(source, name, index).start()

    def pass_on(source, tile, which, first, arriving, leaving):
        part(source, arriving, tile).wait_recv()
        count = SUPER // 2
        lanes = tiles(source)[tile]
        if source in PAIR_FIRST:
            count = count // 2
            unit, start = ((3, 0), (2, count))[which]
            far[source, which, :count] = far[source, which, :count] + paired[
                PAIR_FIRST.index(source), unit, start:start + count
            ]
            part(source, leaving, tile).start()
            return
        far[source, which, :, lanes] = far[source, which, :, lanes] + product[source, 1, first:first + count, lanes]
        part(source, leaving, tile).start()

    def own(source, tile):
        count = SUPER // 2
        lanes = tiles(source)[tile]
        for name in ("minus_a", "plus_b", "minus_b", "plus_a"):
            part(source, name, tile).wait_recv()
        if source in PAIR_FIRST:
            count = count // 2
            place = PAIR_FIRST.index(source)
            for first, one, two in ((0, 0, 3), (count, 1, 2)):
                crossed[source, first:first + count] = (
                    paired[place, 1, first:first + count] + near[source, one, :count] + near[source, two, :count]
                )
            hand_over(source, lanes)
            return
        for first, one, two in ((2 * count, 0, 3), (3 * count, 1, 2)):
            product[source, 0, first:first + count, lanes] = (
                product[source, 0, first:first + count, lanes] + near[source, one, :, lanes] + near[source, two, :, lanes]
            )
        part(source, "cross", tile).start()

    def core_copy(source, lanes=slice(None)):
        where = row_at(*SOURCES[source])
        return remote(
            crossed.at[source, pl.ds(pl.multiple_of((1 - core) * SHARE, SHARE), SHARE), lanes],
            result.at[core, pl.ds(pl.multiple_of(where * SHARE, SHARE), SHARE), lanes],
            core_send.at[source],
            core_recv.at[where],
            ways["core"],
        )

    def pair(source, tile):
        part(source, "cross", tile).wait_recv()
        lanes = tiles(source)[tile]
        half = SUPER // 2
        rows = pl.ds(pl.multiple_of(2 * half + y_lo * half, half), half)
        crossed[source, :, lanes] = crossed[source, :, lanes] + product[source, 0, rows, lanes]
        hand_over(source, lanes)

    def hand_over(source, lanes):
        core_copy(source, lanes).start()
        where = row_at(*SOURCES[source])
        result[core, pl.ds(pl.multiple_of(where * SHARE, SHARE), SHARE), lanes] = crossed[
            source, pl.ds(pl.multiple_of(core * SHARE, SHARE), SHARE), lanes
        ]

    for task in ORDER:
        if task[0] == "arrive":
            arrive(task[1], task[2])
        elif task[0] == "rest":
            first_sends(1, (0, 1, 2, 3))
        elif task[0] == "convert":
            convert_all(task[1] == 1)
        elif task[0] == "product":
            multiply(task[1], task[2])
        elif task[0] == "minus":
            pass_on(task[1], task[2], 1, SUPER // 2, "far_b", "minus_b")
        elif task[0] == "plus":
            pass_on(task[1], task[2], 0, SUPER, "far_a", "plus_a")
        elif task[0] == "first":
            pair_first(task[1], task[2])
        elif task[0] == "own":
            own(task[1], task[2])
        else:
            pair(task[1], task[2])

    own_load(0).wait()
    own_load(1).wait()

    def core_wait(step, carry):
        place = result.at[1 - core, pl.ds(pl.multiple_of(step * SHARE, SHARE), SHARE)]
        pltpu.make_async_copy(place, place, core_recv.at[step]).wait()
        return carry

    lax.fori_loop(0, ROWS, core_wait, 0)

    def tile_of(half, block):
        side, first = (block * SUPER) // half_rows, (block * SUPER) % half_rows
        return result[side, half * SUPER:(half + 1) * SUPER, first:first + SUPER]

    for half in range(2):
        total = jnp.zeros((SUPER, SUPER), jnp.float32)
        for block in range(blocks):
            lanes = slice(block * SUPER, (block + 1) * SUPER)
            t_high, t_low = split(tile_of(half, block))
            p_high, p_low = split(chunk[half, lanes, :] * kept(row * blocks + block, col * 2 + half))
            total += jnp.dot(t_high, p_low, preferred_element_type=jnp.float32)
            total += jnp.dot(t_low, p_high, preferred_element_type=jnp.float32)
            total += jnp.dot(t_high, p_high, preferred_element_type=jnp.float32)
        share = SUPER // ROWS
        for target in range(ROWS):
            mine[target, half] = total[target * share:(target + 1) * share]

    def diag_copy(step):
        target = lax.rem(row + step, ROWS)
        return remote(
            mine.at[target], theirs.at[step], diag_send.at[step], diag_recv.at[step], (target, col)
        )

    for step in range(1, ROWS):
        diag_copy(step).start()

    for half in range(2):
        for block in range(blocks):
            keep = kept(row * blocks + block, col * 2 + half)
            off[half * SUPER:(half + 1) * SUPER, block * SUPER:(block + 1) * SUPER] = tile_of(half, block) * (-keep)
    for index in range(3):
        a_swap(index).wait_send()
    for message in range(len(HEAD)):
        if stays(message) is None:
            head_copy(message).wait_send()
        else:

            @pl.when(jnp.logical_not(stays(message)))
            def _():
                head_copy(message).wait_send()

    for source, half, way in SENDS:
        gather_copy(source, half, way).wait_send()
    for source in range(ROWS):
        for name in PARTS[:6] if source in PAIR_FIRST else PARTS:
            part(source, name).wait_send()
        if source in PAIR_FIRST:
            for unit in range(4):
                pair_copy(source, unit).wait_send()
        core_copy(source).wait_send()

    total = diag[...] + mine[row]
    for step in range(1, ROWS):
        diag_copy(step).wait_recv()
        total += theirs[step]
    diag_out[...] = total
    for step in range(1, ROWS):
        diag_copy(step).wait_send()


def body(ancestor_inv, lower_panel, diag_block_inv, pattern):
    depth, width = ancestor_inv.shape
    width_here = lower_panel.shape[1]
    share = SUPER // ROWS
    half = SUPER // 2
    f32, bf16 = jnp.float32, jnp.bfloat16
    dma = pltpu.SemaphoreType.DMA
    return pl.pallas_call(
        kernel,
        out_shape=(
            jax.ShapeDtypeStruct((width_here, depth), f32),
            jax.ShapeDtypeStruct(diag_block_inv.shape, f32),
        ),
        in_specs=[
            pl.BlockSpec(memory_space=pl.ANY),
            pl.BlockSpec(memory_space=pl.ANY),
            pl.BlockSpec(memory_space=pl.ANY),
            pl.BlockSpec(memory_space=pltpu.VMEM),
        ],
        out_specs=(pl.BlockSpec(memory_space=pltpu.VMEM), pl.BlockSpec(memory_space=pltpu.VMEM)),
        scratch_shapes=[
            pltpu.SMEM(pattern.shape, pattern.dtype),
            pltpu.VMEM((ROWS, 2, 2, SUPER, depth), f32),
            pltpu.VMEM((depth, width), bf16),
            pltpu.VMEM((depth, width), bf16),
            pltpu.VMEM((2 * SUPER, depth), bf16),
            pltpu.VMEM((2 * SUPER, depth), bf16),
            pltpu.VMEM((ROWS, 2, 2 * SUPER, width), f32),
            pltpu.VMEM((ROWS, 2, half, width), f32),
            pltpu.VMEM((ROWS, 4, half, width), f32),
            pltpu.VMEM((ROWS, half, width), f32),
            pltpu.VMEM((len(PAIR_FIRST), 4, half, width), f32),
            pltpu.VMEM((2, width_here, width), f32),
            pltpu.VMEM((2, depth, SUPER), f32),
            pltpu.VMEM((SUPER, depth), f32),
            pltpu.VMEM((len(HEAD), SHARE, depth), f32),
            pltpu.VMEM((ROWS, 2, share, SUPER), f32),
            pltpu.VMEM((ROWS, 2, share, SUPER), f32),
            dma((2,)),
            dma((3,)),
            dma((3,)),
            dma((3,)),
            dma((len(HEAD),)),
            dma((2, 4)),
            dma((len(SENDS),)),
            dma((ROWS, 2, 2)),
            dma((ROWS, 7)),
            dma((ROWS, 7, 3)),
            dma((len(PAIR_FIRST), 4)),
            dma((len(PAIR_FIRST), 4)),
            dma((ROWS,)),
            dma((ROWS,)),
            dma((ROWS,)),
            dma((ROWS,)),
            dma,
        ],
        compiler_params=pltpu.CompilerParams(
            collective_id=0, has_side_effects=True, vmem_limit_bytes=63 * 2**20
        ),
        cost_estimate=pl.CostEstimate(
            flops=6 * depth * width * 16 * 2 * SUPER, bytes_accessed=16 * 2**20, transcendentals=0
        ),
    )(pattern, lower_panel, ancestor_inv, diag_block_inv)


def solution(mesh):
    in_specs = (P("row", "col"), P(None, "col"), P("col", "row", None), P())
    out_specs = (P("col", "row"), P("col", "row", None))
    return jax.shard_map(body, mesh=mesh, in_specs=in_specs, out_specs=out_specs, check_vma=False)
```

```python
import jax
import jax.numpy as jnp
from jax import lax
from jax.experimental import pallas as pl
from jax.experimental.pallas import tpu as pltpu
from jax.sharding import PartitionSpec as P

SUPER = 128
MESH = pl.DeviceIdType.MESH
RING = 4
ROWS = 8
SHARE = 32

SOURCES = ((0, 0), (0, 1), (-1, 0), (1, 0), (-1, 1), (1, 1), (2, 0), (2, 1))
HEAD = tuple((dx, dy, place) for dx, place in ((2, (0, 0)), (0, (1, 0)), (1, (0, 1)), (-1, (1, 1))) for dy in range(2))


def forwards(source, half):
    dz, dy = SOURCES[source]
    out = []
    if dz == 0:
        if dy == 0:
            out.append(("yh", SOURCES.index((0, 1))))
        out.append(("z+", SOURCES.index((-1, dy))))
        out.append(("z-", SOURCES.index((1, dy))))
    if dz == -1 and half == 0:
        out.append(("z+", SOURCES.index((2, dy))))
    if dz == 1 and half == 1:
        out.append(("z-", SOURCES.index((2, dy))))
    out.append(("core", source))
    return out


SENDS = {}
for _source in range(ROWS):
    for _half in range(2):
        for _way, _ in forwards(_source, _half):
            SENDS[(_source, _half, _way)] = len(SENDS)

ORDER = (
    ("convert", 0),
    ("rest", 1),
    ("convert", 1),
    ("product", 0, 0),
    ("product", 0, 1),
    ("minus", 0, 0),
    ("plus", 0, 0),
    ("arrive", 2, 0),
    ("arrive", 3, 0),
    ("arrive", 1, 0),
    ("own", 0, 0),
    ("product", 2, 0),
    ("product", 3, 0),
    ("product", 1, 0),
    ("pair", 0, 0),
    ("arrive", 2, 1),
    ("arrive", 3, 1),
    ("arrive", 1, 1),
    ("product", 2, 1),
    ("minus", 2, 0),
    ("plus", 2, 0),
    ("product", 3, 1),
    ("minus", 3, 0),
    ("plus", 3, 0),
    ("product", 1, 1),
    ("minus", 1, 0),
    ("plus", 1, 0),
    ("arrive", 5, 0),
    ("arrive", 6, 0),
    ("own", 2, 0),
    ("product", 5, 0),
    ("product", 6, 0),
    ("own", 3, 0),
    ("pair", 2, 0),
    ("first", 5, 0),
    ("arrive", 4, 0),
    ("arrive", 6, 1),
    ("first", 5, 1),
    ("own", 1, 0),
    ("product", 4, 0),
    ("pair", 3, 0),
    ("product", 6, 1),
    ("minus", 6, 0),
    ("plus", 6, 0),
    ("pair", 1, 0),
    ("first", 4, 0),
    ("arrive", 4, 1),
    ("arrive", 5, 1),
    ("first", 4, 1),
    ("product", 4, 1),
    ("own", 6, 0),
    ("product", 5, 1),
    ("first", 4, 2),
    ("minus", 4, 0),
    ("arrive", 7, 0),
    ("first", 4, 3),
    ("arrive", 7, 1),
    ("plus", 4, 0),
    ("product", 7, 0),
    ("pair", 6, 0),
    ("product", 7, 1),
    ("minus", 7, 0),
    ("plus", 7, 0),
    ("own", 4, 0),
    ("minus", 7, 1),
    ("plus", 7, 1),
    ("first", 5, 2),
    ("minus", 5, 0),
    ("minus", 7, 2),
    ("plus", 7, 2),
    ("first", 5, 3),
    ("plus", 5, 0),
    ("own", 7, 0),
    ("own", 7, 1),
    ("pair", 7, 0),
    ("pair", 7, 1),
    ("own", 7, 2),
    ("own", 5, 0),
    ("pair", 7, 2),
)
TILES = (1, 1, 1, 1, 1, 1, 1, 3)
PAIR_FIRST = (4, 5)
PARTS = ("far_a", "far_b", "minus_a", "plus_b", "minus_b", "plus_a", "cross")


def split(value):
    high = value.astype(jnp.bfloat16)
    low = (value - high.astype(jnp.float32)).astype(jnp.bfloat16)
    return high, low


def kernel(
    pattern_in, panel, ancestor, diag, off, diag_out,
    pattern,
    gathered, a_high, a_low, m_high, m_low, product, far, near, crossed, paired, result, chunk, turned, pieces, mine, theirs,
    chunk_sem, a_sem, a_send, a_recv, head_send, head_recv, gather_send, gather_recv, part_send, part_recv, pair_send, pair_recv,
    core_send, core_recv, diag_send, diag_recv, pattern_sem,
):
    row, col = lax.axis_index("row"), lax.axis_index("col")
    y_hi, z = row // RING, lax.rem(row, RING)
    x, y_lo, core = col // 4, lax.rem(col // 2, 2), lax.rem(col, 2)
    rows_here, cols_here = ancestor.shape
    depth = rows_here
    blocks = depth // SUPER
    half_rows = rows_here // 2

    def col_at(dx, dy, target_core):
        nx = lax.rem(x + (dx + RING), RING)
        ny = 1 - y_lo if dy else y_lo
        return nx * 4 + ny * 2 + target_core

    def row_at(dz, dy):
        nz = lax.rem(z + (dz + RING), RING)
        return (1 - y_hi if dy else y_hi) * RING + nz

    ways = {
        "x+": (row, col_at(1, 0, core)),
        "x-": (row, col_at(-1, 0, core)),
        "y": (row, col_at(0, 1, core)),
        "core": (row, col_at(0, 0, 1 - core)),
        "z+": (row_at(1, 0), col),
        "z-": (row_at(-1, 0), col),
        "yh": (row_at(0, 1), col),
    }

    def remote(source, target, send, recv, device):
        return pltpu.make_async_remote_copy(
            src_ref=source, dst_ref=target, send_sem=send, recv_sem=recv, device_id=device, device_id_type=MESH
        )

    pattern_copy = pltpu.make_async_copy(pattern_in, pattern, pattern_sem)
    pattern_copy.start()

    barrier = pltpu.get_barrier_semaphore()

    def greet(device):
        pl.semaphore_signal(barrier, inc=1, device_id=device, device_id_type=MESH)

    def greet_row(step, carry):
        greet((row, lax.rem(col + step, 16)))
        return carry

    lax.fori_loop(1, 16, greet_row, 0)
    for way in ("z+", "z-", "yh"):
        greet(ways[way])

    def chunk_load(message):
        dx, dy, _ = HEAD[message]
        chip = col_at(dx, dy, 0) // 2
        rows = pl.ds(pl.multiple_of(chip * depth, SUPER), depth)
        lanes = pl.ds(pl.multiple_of((row // 4) * SUPER, SUPER), SUPER)
        return pltpu.make_async_copy(panel.at[rows, lanes], chunk.at[message % 2], chunk_sem.at[message % 2])

    def a_rows(which, part):
        return ancestor.at[pl.ds(pl.multiple_of(which * half_rows + part * 256, 256), 256)]

    own_place = ((2, 0), (2, 1), (3, 0))
    other_place = ((3, 1), (4, 0), (4, 1))

    def a_load(part):
        slot, half = own_place[part]
        return pltpu.make_async_copy(a_rows(core, part), product.at[slot, half], a_sem.at[part])

    def a_swap(part):
        slot, half = other_place[part]
        return remote(
            a_rows(1 - core, part), product.at[slot, half], a_send.at[part], a_recv.at[part], ways["core"]
        )

    chunk_load(0).start()
    chunk_load(1).start()
    for part in range(3):
        a_load(part).start()

    def kept(block_row, column):
        return pattern[block_row, column].astype(jnp.float32)

    def head_copy(message):
        dx, dy, (target_core, half) = HEAD[message]
        piece = y_lo * 2 + core
        return remote(
            pieces.at[message],
            gathered.at[0, target_core, half, pl.ds(pl.multiple_of(piece * SHARE, SHARE), SHARE)],
            head_send.at[message],
            head_recv.at[half, piece],
            (row, col_at(dx, dy, target_core)),
        )

    def head_stay(message):
        _, _, (target_core, half) = HEAD[message]
        piece = y_lo * 2 + core
        return pltpu.make_async_copy(
            pieces.at[message],
            gathered.at[0, target_core, half, pl.ds(pl.multiple_of(piece * SHARE, SHARE), SHARE)],
            head_recv.at[half, piece],
        )

    def stays(message):
        dx, dy, (target_core, _) = HEAD[message]
        return core == target_core if (dx, dy) == (0, 0) else None

    def turn(message):
        dx, dy, _ = HEAD[message]
        chip = col_at(dx, dy, 0) // 2
        chunk_load(message).wait()

        def block_turn(block, carry):
            rows = pl.ds(pl.multiple_of(block * SUPER, SUPER), SUPER)
            tile = chunk[message % 2, rows, :] * kept(chip * blocks + block, col * 2 + row // 4)
            turned[:, rows] = tile.T
            return carry

        lax.fori_loop(0, blocks, block_turn, 0, unroll=6)
        if message + 2 < len(HEAD):
            chunk_load(message + 2).start()
        pieces[message] = turned[pl.ds(pl.multiple_of(lax.rem(row, 4) * SHARE, SHARE), SHARE), :]

    def gather_copy(source, half, way, rows=slice(None)):
        target = dict(forwards(source, half))[way]
        return remote(
            gathered.at[source, core, half, rows],
            gathered.at[target, core, half, rows],
            gather_send.at[SENDS[(source, half, way)]],
            gather_recv.at[target, core, half],
            ways[way],
        )

    def landed(source, which, half):
        place = gathered.at[source, which, half]
        pltpu.make_async_copy(place, place, gather_recv.at[source, which, half]).wait()

    def arrive(source, half):
        if source > 0:
            landed(source, core, half)
            for way, _ in forwards(source, half):
                gather_copy(source, half, way).start()
            return
        first_sends(half, (0, 1, 2, 3))

    def first_sends(half, steps):
        for step in steps:
            piece = ((1 - y_lo) if step >= 2 else y_lo) * 2 + step % 2
            rows = pl.ds(pl.multiple_of(piece * SHARE, SHARE), SHARE)
            place = gathered.at[0, core, half, rows]
            pltpu.make_async_copy(place, place, head_recv.at[half, piece]).wait()
            for way, _ in forwards(0, half):
                gather_copy(0, half, way, rows).start()

    pattern_copy.wait()
    turn(0)
    pl.semaphore_wait(barrier, 18)
    for part in range(3):
        a_swap(part).start()
    for message in range(len(HEAD)):
        if message > 0:
            turn(message)
        if stays(message) is None:
            head_copy(message).start()
        else:

            @pl.when(stays(message))
            def _():
                head_stay(message).start()

            @pl.when(jnp.logical_not(stays(message)))
            def _():
                head_copy(message).start()

        if message == 3:
            first_sends(0, (0, 1))
        if message == 7:
            first_sends(0, (2, 3))

    def own_load(half):
        rows = pl.ds(pl.multiple_of(row * depth, SUPER), depth)
        return pltpu.make_async_copy(
            panel.at[rows, pl.ds(half * SUPER, SUPER)], chunk.at[half], chunk_sem.at[half]
        )

    own_load(0).start()
    own_load(1).start()

    def convert(place, part, offset):
        slot, half = place[part]
        for step in range(2):
            for side in range(cols_here // 256):
                tile = product[slot, half, step * SUPER:(step + 1) * SUPER, side * 256:(side + 1) * 256].T
                high, low = split(tile)
                rows = pl.ds(pl.multiple_of(offset + side * 256, 256), 256)
                lanes = slice(part * 256 + step * SUPER, part * 256 + (step + 1) * SUPER)
                a_high[rows, lanes] = high
                a_low[rows, lanes] = low

    def convert_all(swapped):
        for part in range(3):
            if swapped:
                a_swap(part).wait_recv()
                convert(other_place, part, (1 - core) * cols_here)
            else:
                a_load(part).wait()
                convert(own_place, part, core * cols_here)

    def tiles(source):
        count = TILES[source]
        return [slice(t * half_rows // count, (t + 1) * half_rows // count) for t in range(count)]

    def part(source, name, tile=None):
        lanes = slice(None) if tile is None else tiles(source)[tile]
        index = PARTS.index(name)
        half = SUPER // 2
        if source in PAIR_FIRST:
            count = half // 2
            held = paired.at[PAIR_FIRST.index(source)]
            block, target, way = {
                "far_a": lambda: (held.at[0, pl.ds(0, count)], far.at[source, 0, pl.ds(0, count)], "x+"),
                "far_b": lambda: (held.at[0, pl.ds(count, count)], far.at[source, 1, pl.ds(0, count)], "x-"),
                "minus_a": lambda: (held.at[2, pl.ds(0, count)], near.at[source, 0, pl.ds(0, count)], "x-"),
                "plus_b": lambda: (held.at[3, pl.ds(count, count)], near.at[source, 1, pl.ds(0, count)], "x+"),
                "minus_b": lambda: (far.at[source, 1, pl.ds(0, count)], near.at[source, 2, pl.ds(0, count)], "x-"),
                "plus_a": lambda: (far.at[source, 0, pl.ds(0, count)], near.at[source, 3, pl.ds(0, count)], "x+"),
            }[name]()
            return remote(
                block, target, part_send.at[source, index], part_recv.at[source, index, 0], ways[way]
            )
        first, second = product.at[source, 0], product.at[source, 1]
        block, target, way = {
            "far_a": lambda: (first.at[pl.ds(0, half), lanes], far.at[source, 0, :, lanes], "x+"),
            "far_b": lambda: (first.at[pl.ds(half, half), lanes], far.at[source, 1, :, lanes], "x-"),
            "minus_a": lambda: (second.at[pl.ds(0, half), lanes], near.at[source, 0, :, lanes], "x-"),
            "plus_b": lambda: (second.at[pl.ds(3 * half, half), lanes], near.at[source, 1, :, lanes], "x+"),
            "minus_b": lambda: (far.at[source, 1, :, lanes], near.at[source, 2, :, lanes], "x-"),
            "plus_a": lambda: (far.at[source, 0, :, lanes], near.at[source, 3, :, lanes], "x+"),
            "cross": lambda: (
                first.at[pl.ds(pl.multiple_of(2 * half + (1 - y_lo) * half, half), half), lanes],
                crossed.at[source, :, lanes],
                "y",
            ),
        }[name]()
        return remote(
            block, target, part_send.at[source, index], part_recv.at[source, index, tile or 0], ways[way]
        )

    def pair_copy(source, unit):
        half = SUPER // 2
        rows = pl.ds(pl.multiple_of((unit % 2) * SUPER + (1 - y_lo) * half, half), half)
        place = PAIR_FIRST.index(source)
        return remote(
            product.at[source, unit // 2, rows],
            paired.at[place, unit],
            pair_send.at[place, unit],
            pair_recv.at[place, unit],
            ways["y"],
        )

    def pair_first(source, unit):
        pair_copy(source, unit).wait_recv()
        half = SUPER // 2
        rows = pl.ds(pl.multiple_of((unit % 2) * SUPER + y_lo * half, half), half)
        place = PAIR_FIRST.index(source)
        paired[place, unit] = paired[place, unit] + product[source, unit // 2, rows, :]
        for name in (("far_a", "far_b"), (), ("minus_a",), ("plus_b",))[unit]:
            part(source, name, 0).start()

    def multiply(source, half):
        landed(source, 1 - core, half)
        for which in range(2):
            def prepare(step, carry):
                rows = pl.ds(pl.multiple_of(step * 32, 32), 32)
                out = pl.ds(pl.multiple_of(which * SUPER + step * 32, 32), 32)
                high, low = split(gathered[source, which, half, rows, :])
                m_high[out, :] = high
                m_low[out, :] = low
                return carry

            lax.fori_loop(0, SUPER // 32, prepare, 0, unroll=2)

        def tile(step, carry):
            lanes = pl.ds(pl.multiple_of(step * 256, 256), 256)
            high = a_high[:, lanes]
            total = jnp.dot(m_low[...], high, preferred_element_type=jnp.float32)
            total += jnp.dot(m_high[...], a_low[:, lanes], preferred_element_type=jnp.float32)
            total += jnp.dot(m_high[...], high, preferred_element_type=jnp.float32)
            product[source, half, :, lanes] = total
            return carry

        lax.fori_loop(0, half_rows // 256, tile, 0)
        if source in PAIR_FIRST:
            for unit in (2 * half, 2 * half + 1):
                pair_copy(source, unit).start()
            return
        for index in range(TILES[source]):
            for name in ("far_a", "far_b") if half == 0 else ("minus_a", "plus_b"):
                part(source, name, index).start()

    def pass_on(source, tile, which, first, arriving, leaving):
        part(source, arriving, tile).wait_recv()
        count = SUPER // 2
        lanes = tiles(source)[tile]
        if source in PAIR_FIRST:
            count = count // 2
            unit, start = ((3, 0), (2, count))[which]
            far[source, which, :count] = far[source, which, :count] + paired[
                PAIR_FIRST.index(source), unit, start:start + count
            ]
            part(source, leaving, tile).start()
            return
        far[source, which, :, lanes] = far[source, which, :, lanes] + product[source, 1, first:first + count, lanes]
        part(source, leaving, tile).start()

    def own(source, tile):
        count = SUPER // 2
        lanes = tiles(source)[tile]
        for name in ("minus_a", "plus_b", "minus_b", "plus_a"):
            part(source, name, tile).wait_recv()
        if source in PAIR_FIRST:
            count = count // 2
            place = PAIR_FIRST.index(source)
            for first, one, two in ((0, 0, 3), (count, 1, 2)):
                crossed[source, first:first + count] = (
                    paired[place, 1, first:first + count] + near[source, one, :count] + near[source, two, :count]
                )
            hand_over(source, lanes)
            return
        for first, one, two in ((2 * count, 0, 3), (3 * count, 1, 2)):
            product[source, 0, first:first + count, lanes] = (
                product[source, 0, first:first + count, lanes] + near[source, one, :, lanes] + near[source, two, :, lanes]
            )
        part(source, "cross", tile).start()

    def core_copy(source, lanes=slice(None)):
        where = row_at(*SOURCES[source])
        return remote(
            crossed.at[source, pl.ds(pl.multiple_of((1 - core) * SHARE, SHARE), SHARE), lanes],
            result.at[core, pl.ds(pl.multiple_of(where * SHARE, SHARE), SHARE), lanes],
            core_send.at[source],
            core_recv.at[where],
            ways["core"],
        )

    def pair(source, tile):
        part(source, "cross", tile).wait_recv()
        lanes = tiles(source)[tile]
        half = SUPER // 2
        rows = pl.ds(pl.multiple_of(2 * half + y_lo * half, half), half)
        crossed[source, :, lanes] = crossed[source, :, lanes] + product[source, 0, rows, lanes]
        hand_over(source, lanes)

    def hand_over(source, lanes):
        core_copy(source, lanes).start()
        where = row_at(*SOURCES[source])
        result[core, pl.ds(pl.multiple_of(where * SHARE, SHARE), SHARE), lanes] = crossed[
            source, pl.ds(pl.multiple_of(core * SHARE, SHARE), SHARE), lanes
        ]

    for task in ORDER:
        if task[0] == "arrive":
            arrive(task[1], task[2])
        elif task[0] == "rest":
            first_sends(1, (0, 1, 2, 3))
        elif task[0] == "convert":
            convert_all(task[1] == 1)
        elif task[0] == "product":
            multiply(task[1], task[2])
        elif task[0] == "minus":
            pass_on(task[1], task[2], 1, SUPER // 2, "far_b", "minus_b")
        elif task[0] == "plus":
            pass_on(task[1], task[2], 0, SUPER, "far_a", "plus_a")
        elif task[0] == "first":
            pair_first(task[1], task[2])
        elif task[0] == "own":
            own(task[1], task[2])
        else:
            pair(task[1], task[2])

    own_load(0).wait()
    own_load(1).wait()

    def core_wait(step, carry):
        place = result.at[1 - core, pl.ds(pl.multiple_of(step * SHARE, SHARE), SHARE)]
        pltpu.make_async_copy(place, place, core_recv.at[step]).wait()
        return carry

    lax.fori_loop(0, ROWS, core_wait, 0)

    def tile_of(half, block):
        side, first = (block * SUPER) // half_rows, (block * SUPER) % half_rows
        return result[side, half * SUPER:(half + 1) * SUPER, first:first + SUPER]

    for half in range(2):
        total = jnp.zeros((SUPER, SUPER), jnp.float32)
        for block in range(blocks):
            lanes = slice(block * SUPER, (block + 1) * SUPER)
            t_high, t_low = split(tile_of(half, block))
            p_high, p_low = split(chunk[half, lanes, :] * kept(row * blocks + block, col * 2 + half))
            total += jnp.dot(t_high, p_low, preferred_element_type=jnp.float32)
            total += jnp.dot(t_low, p_high, preferred_element_type=jnp.float32)
            total += jnp.dot(t_high, p_high, preferred_element_type=jnp.float32)
        share = SUPER // ROWS
        for target in range(ROWS):
            mine[target, half] = total[target * share:(target + 1) * share]

    def diag_copy(step):
        target = lax.rem(row + step, ROWS)
        return remote(
            mine.at[target], theirs.at[step], diag_send.at[step], diag_recv.at[step], (target, col)
        )

    for step in range(1, ROWS):
        diag_copy(step).start()

    for half in range(2):
        for block in range(blocks):
            keep = kept(row * blocks + block, col * 2 + half)
            off[half * SUPER:(half + 1) * SUPER, block * SUPER:(block + 1) * SUPER] = tile_of(half, block) * (-keep)
    for index in range(3):
        a_swap(index).wait_send()
    for message in range(len(HEAD)):
        if stays(message) is None:
            head_copy(message).wait_send()
        else:

            @pl.when(jnp.logical_not(stays(message)))
            def _():
                head_copy(message).wait_send()

    for source, half, way in SENDS:
        gather_copy(source, half, way).wait_send()
    for source in range(ROWS):
        for name in PARTS[:6] if source in PAIR_FIRST else PARTS:
            part(source, name).wait_send()
        if source in PAIR_FIRST:
            for unit in range(4):
                pair_copy(source, unit).wait_send()
        core_copy(source).wait_send()

    total = diag[...] + mine[row]
    for step in range(1, ROWS):
        diag_copy(step).wait_recv()
        total += theirs[step]
    diag_out[...] = total
    for step in range(1, ROWS):
        diag_copy(step).wait_send()


def body(ancestor_inv, lower_panel, diag_block_inv, pattern):
    depth, width = ancestor_inv.shape
    width_here = lower_panel.shape[1]
    share = SUPER // ROWS
    half = SUPER // 2
    f32, bf16 = jnp.float32, jnp.bfloat16
    dma = pltpu.SemaphoreType.DMA
    return pl.pallas_call(
        kernel,
        out_shape=(
            jax.ShapeDtypeStruct((width_here, depth), f32),
            jax.ShapeDtypeStruct(diag_block_inv.shape, f32),
        ),
        in_specs=[
            pl.BlockSpec(memory_space=pl.ANY),
            pl.BlockSpec(memory_space=pl.ANY),
            pl.BlockSpec(memory_space=pl.ANY),
            pl.BlockSpec(memory_space=pltpu.VMEM),
        ],
        out_specs=(pl.BlockSpec(memory_space=pltpu.VMEM), pl.BlockSpec(memory_space=pltpu.VMEM)),
        scratch_shapes=[
            pltpu.SMEM(pattern.shape, pattern.dtype),
            pltpu.VMEM((ROWS, 2, 2, SUPER, depth), f32),
            pltpu.VMEM((depth, width), bf16),
            pltpu.VMEM((depth, width), bf16),
            pltpu.VMEM((2 * SUPER, depth), bf16),
            pltpu.VMEM((2 * SUPER, depth), bf16),
            pltpu.VMEM((ROWS, 2, 2 * SUPER, width), f32),
            pltpu.VMEM((ROWS, 2, half, width), f32),
            pltpu.VMEM((ROWS, 4, half, width), f32),
            pltpu.VMEM((ROWS, half, width), f32),
            pltpu.VMEM((len(PAIR_FIRST), 4, half, width), f32),
            pltpu.VMEM((2, width_here, width), f32),
            pltpu.VMEM((2, depth, SUPER), f32),
            pltpu.VMEM((SUPER, depth), f32),
            pltpu.VMEM((len(HEAD), SHARE, depth), f32),
            pltpu.VMEM((ROWS, 2, share, SUPER), f32),
            pltpu.VMEM((ROWS, 2, share, SUPER), f32),
            dma((2,)),
            dma((3,)),
            dma((3,)),
            dma((3,)),
            dma((len(HEAD),)),
            dma((2, 4)),
            dma((len(SENDS),)),
            dma((ROWS, 2, 2)),
            dma((ROWS, 7)),
            dma((ROWS, 7, 3)),
            dma((len(PAIR_FIRST), 4)),
            dma((len(PAIR_FIRST), 4)),
            dma((ROWS,)),
            dma((ROWS,)),
            dma((ROWS,)),
            dma((ROWS,)),
            dma,
        ],
        compiler_params=pltpu.CompilerParams(
            collective_id=0, has_side_effects=True, vmem_limit_bytes=63 * 2**20
        ),
        cost_estimate=pl.CostEstimate(
            flops=6 * depth * width * 16 * 2 * SUPER, bytes_accessed=16 * 2**20, transcendentals=0
        ),
    )(pattern, lower_panel, ancestor_inv, diag_block_inv)


def solution(mesh):
    in_specs = (P("row", "col"), P(None, "col"), P("col", "row", None), P())
    out_specs = (P("col", "row"), P("col", "row", None))
    return jax.shard_map(body, mesh=mesh, in_specs=in_specs, out_specs=out_specs, check_vma=False)
```
